512 devices in a mesh: box: 64 (over x, z_hi, y, core), freq: 8 (over z_lo).
Axes of the slice: x: 4, y: 4, z: 16 (z_hi: 2, z_lo: 8; z = z_hi * 8 + z_lo), core: 2. Of those that a mesh axis runs over, the one named last changes fastest.
Arguments:
- spectra_fine: bfloat16 [4096, 2, 8, 1024], P(('box', 'freq')), may hold values from -6 to 6
- spectra_coarse: bfloat16 [512, 2, 8, 1024], P(('box', 'freq')), may hold values from -6 to 6
- kernel_table: bfloat16 [26, 2, 8, 8, 1024], P(None, None, None, None, 'freq'), may hold values from -0.3125 to 0.3125
- lists_fine: int32 [4096, 26], P('box'), may hold values from -1 to 4095, as said below
- lists_coarse: int32 [512, 26], P('box'), may hold values from -1 to 511, as said below
- live_counts: int32 [64, 2], P('box'), may hold values from 4 to 64, as said below
Outputs:
- potentials_fine: bfloat16 [4096, 2, 8, 1024], P('box', None, None, 'freq')
- potentials_coarse: bfloat16 [512, 2, 8, 1024], P('box', None, None, 'freq')
The draws below stay inside these ranges and needn't reach their ends.
Inputs may be any that keep to these rules, and one draw needn't show every extreme that they name: `lists_fine`: each entry is -1 or a group whose Morton index differs from the target's by at most 16; that distance is reached. `lists_coarse`: each entry is -1 or a group whose Morton index differs from the target's by at most 2; that distance is reached. `live_counts`: column 0 lies in 32 to 64, column 1 in 4 to 8; each column reaches its largest value on some index.
All inputs are finite; a program needn't handle non-finite values.
Results may differ from the reference program's by a relative error of at most 0.007.
Values may be sent and summed in bfloat16 or wider, within the bound.
A program may use at most 64 MiB of HBM per device.

```python
import jax
import jax.numpy as jnp
from jax import lax

BOXES = 64
COARSE = 8
SLOTS = 26
FREQ = 1024
RIM_FINE = 16
RIM_COARSE = 2
GROUPS_FINE = 4096
GROUPS_COARSE = 512
N_BOX = 64


def neighbour_lists(key, total_rows, rim_width):
    near_key, empty_key = jax.random.split(key)
    target = jnp.arange(total_rows, dtype=jnp.int32)[:, None]
    source = target + jax.random.randint(near_key, (total_rows, SLOTS), -rim_width, rim_width + 1, dtype=jnp.int32)
    vacant = jax.random.randint(empty_key, (total_rows, SLOTS), 0, 4, dtype=jnp.int32) == 0
    inside = (source >= 0) & (source < total_rows) & jnp.logical_not(vacant)
    return jnp.where(inside, source, -1).astype(jnp.int32)


def draw_lists_fine(key, part):
    key = jax.random.fold_in(key, 11)
    return neighbour_lists(key, GROUPS_FINE, RIM_FINE)


def draw_lists_coarse(key, part):
    key = jax.random.fold_in(key, 12)
    return neighbour_lists(key, GROUPS_COARSE, RIM_COARSE)


def draw_live_counts(key, part):
    key = jax.random.fold_in(key, 13)
    fine_key, coarse_key, fine_pick, coarse_pick = jax.random.split(key, 4)
    fine_count = jax.random.randint(fine_key, (N_BOX,), BOXES // 2, BOXES + 1, dtype=jnp.int32)
    coarse_count = jax.random.randint(coarse_key, (N_BOX,), COARSE // 2, COARSE + 1, dtype=jnp.int32)
    fine_count = fine_count.at[jax.random.randint(fine_pick, (), 0, N_BOX, dtype=jnp.int32)].set(BOXES)
    coarse_count = coarse_count.at[jax.random.randint(coarse_pick, (), 0, N_BOX, dtype=jnp.int32)].set(COARSE)
    return jnp.stack([fine_count, coarse_count], 1).astype(jnp.int32)


def block_levels(rng, extent, shards, low, top_value):
    def one(dim, blocks):
        heights = jax.random.uniform(jax.random.fold_in(jax.random.fold_in(rng, 6), dim), (blocks,), jnp.float32, low / len(shards), top_value / len(shards))
        return jnp.repeat(jnp.exp(heights), extent[dim] // blocks).reshape((-1,) + (1,) * (len(extent) - dim - 1))

    factor_of = one(*shards[0])
    for cut in shards[1:]:
        factor_of = factor_of * one(*cut)
    return factor_of


def scatter_about(stream_key, shape, deviation, most, pieces=(), held_as=jnp.bfloat16):
    drawn = deviation * jax.random.normal(stream_key, shape, jnp.float32)
    if pieces:
        drawn = drawn * block_levels(stream_key, shape, pieces, -0.22, 0.18)
    return jnp.clip(drawn, -most, most).astype(held_as)


def setup_inputs(seed: int = 0) -> dict:
    seeds = jax.random.split(jax.random.key(seed), 7)
    return {
        "spectra_fine": scatter_about(seeds[0], (GROUPS_FINE, 2, 8, FREQ), 1.0, 6.0, ((0, 512),)),
        "spectra_coarse": scatter_about(seeds[1], (GROUPS_COARSE, 2, 8, FREQ), 1.0, 6.0, ((0, 512),)),
        "kernel_table": scatter_about(seeds[2], (SLOTS, 2, 8, 8, FREQ), (16 * SLOTS) ** -0.5, 0.3125, ((4, 8),)),
        "lists_fine": draw_lists_fine(jax.random.fold_in(seeds[6], 71), 0),
        "lists_coarse": draw_lists_coarse(jax.random.fold_in(seeds[6], 71), 0),
        "live_counts": draw_live_counts(jax.random.fold_in(seeds[6], 71), 0),
    }


def level_pass(spectra, lists, counts_column, kernel_table, level_scale, group_count):
    total_rows = spectra.shape[0]
    position = jnp.arange(total_rows, dtype=jnp.int32)
    local_place = position % group_count
    live_here = counts_column[position // group_count]
    lower_live = live_here // 2
    alive_mask = (local_place < lower_live) | (local_place >= group_count - (live_here - lower_live))
    masked = jnp.where(alive_mask[:, None, None, None], spectra, jnp.zeros_like(spectra))
    padded = jnp.concatenate([masked, jnp.zeros((1,) + masked.shape[1:], masked.dtype)], 0)
    source_index = jnp.where(lists >= 0, lists, total_rows).astype(jnp.int32)
    blocks = 8
    block_rows = total_rows // blocks
    width = spectra.shape[3]

    def one_block(first_row):
        block_index = lax.dynamic_slice_in_dim(source_index, first_row, block_rows, 0)

        def one_slot(totals, slot_item):
            kernel_slot, column = slot_item
            picked = padded[column].astype(jnp.float32)
            kernel_slot = kernel_slot.astype(jnp.float32)
            real_part = jnp.einsum('rif,oif->rof', picked[:, 0], kernel_slot[0]) - jnp.einsum('rif,oif->rof', picked[:, 1], kernel_slot[1])
            imag_part = jnp.einsum('rif,oif->rof', picked[:, 1], kernel_slot[0]) + jnp.einsum('rif,oif->rof', picked[:, 0], kernel_slot[1])
            return (totals[0] + real_part, totals[1] + imag_part), None

        zeros_block = jnp.zeros((block_rows, 8, width), jnp.float32)
        (real_sum, imag_sum), _ = lax.scan(one_slot, (zeros_block, zeros_block), (kernel_table, block_index.T))
        return jnp.stack([real_sum, imag_sum], 1)

    starts = jnp.arange(blocks, dtype=jnp.int32) * block_rows
    result = lax.map(one_block, starts).reshape((total_rows, 2, 8, width))
    result = level_scale * result
    result = jnp.where(alive_mask[:, None, None, None], result, jnp.zeros_like(result))
    return result.astype(jnp.bfloat16)


def reference(spectra_fine, spectra_coarse, kernel_table, lists_fine, lists_coarse, live_counts):
    potentials_fine = level_pass(spectra_fine, lists_fine, live_counts[:, 0], kernel_table, 1.0, BOXES)
    potentials_coarse = level_pass(spectra_coarse, lists_coarse, live_counts[:, 1], kernel_table, 0.5, COARSE)
    return potentials_fine, potentials_coarse
```

```python
import functools

import jax
import jax.numpy as jnp
from jax import lax
from jax.experimental import pallas as pl
from jax.experimental.pallas import tpu as pltpu
from jax.sharding import PartitionSpec as P

RIM_FINE = 16
RIM_COARSE = 2
LANES = 128
BAND = 16
BANDS = LANES // BAND
PAIRS = BANDS // 2
WIDE = 2 * 8 * BAND


def swap_blocks(planes):
    block = lax.broadcasted_iota(jnp.int32, planes[0].shape, 1) // BAND
    planes = list(planes)
    for step in (4, 2, 1):
        upper = (block & step) != 0
        for p in range(8):
            if p & step == 0:
                first, second = planes[p], planes[p + step]
                planes[p] = jnp.where(upper, pltpu.roll(second, BAND * step, 1), first)
                planes[p + step] = jnp.where(upper, second, pltpu.roll(first, LANES - BAND * step, 1))
    return planes


def interleave():
    row = lax.broadcasted_iota(jnp.int32, (WIDE, WIDE), 0)
    lane = lax.broadcasted_iota(jnp.int32, (WIDE, WIDE), 1)
    hit = (row // BAND == lane % BAND) & (row % BAND == lane // BAND)
    return jnp.where(hit, 1.0, 0.0).astype(jnp.bfloat16)


def by_band(parts, permutation):
    planes = []
    for part in parts:
        turned = jnp.swapaxes(part, 0, 1)
        planes.append(swap_blocks([turned[i] for i in range(8)]))
    stacked = jnp.concatenate(
        [jnp.concatenate([planes[0][g], planes[1][g]], axis=1) for g in range(BANDS)], axis=0
    ).astype(jnp.bfloat16)
    return jnp.dot(stacked, permutation, preferred_element_type=jnp.float32).astype(jnp.bfloat16)


def alive(place, count, live):
    lower = live // 2
    return (place < lower) | (place >= count - (live - lower))


def kernel(
    n_box,
    n_freq,
    live_ref,
    fine_ref,
    coarse_ref,
    table_ref,
    lists_fine_ref,
    lists_coarse_ref,
    out_fine_ref,
    out_coarse_ref,
    outbox,
    outbox_coarse,
    held,
    held_coarse,
    picks,
    weights,
    gathered,
    sums,
    send_sem,
    recv_sem,
    rim_send,
    rim_recv,
    coarse_send,
    coarse_recv,
    coarse_rim_send,
    coarse_rim_recv,
):
    box = lax.axis_index("box")
    col = lax.axis_index("freq")
    above = lax.rem(box + 1, n_box)
    below = lax.rem(box + n_box - 1, n_box)
    slots = table_ref.shape[0]
    groups = lists_fine_ref.shape[0]
    coarse_groups = lists_coarse_ref.shape[0]
    own = fine_ref.shape[0]
    rows = groups + 16
    live_fine = live_ref[0, 0]
    live_coarse = live_ref[0, 1]
    order = (4, 3, 5, 2, 6, 1, 7)

    barrier = pltpu.get_barrier_semaphore()
    for step in range(1, n_freq):
        pl.semaphore_signal(barrier, inc=1, device_id={"freq": lax.rem(col + step, n_freq)})
    for other in (above, below):
        pl.semaphore_signal(barrier, inc=1, device_id={"box": other})

    permutation = interleave()

    place = col * own + lax.broadcasted_iota(jnp.int32, (own, 8, LANES), 0)
    fine_alive = alive(place, groups, live_fine)
    coarse_alive = alive(jnp.full((16, LANES), col, jnp.int32), coarse_groups, live_coarse)

    def cut(j, carry):
        lanes = pl.ds(pl.multiple_of(j * LANES, LANES), LANES)
        parts = [
            jnp.where(fine_alive, fine_ref[:, c, :, lanes].astype(jnp.float32), 0.0) for c in range(2)
        ]
        outbox[j] = by_band(parts, permutation).reshape(PAIRS, 2 * own, WIDE)
        both = jnp.concatenate(
            [coarse_ref[0, c, :, lanes].astype(jnp.float32) for c in range(2)], axis=0
        )
        outbox_coarse[j] = jnp.where(coarse_alive, both, 0.0).astype(jnp.bfloat16)
        return carry

    lax.fori_loop(0, n_freq, cut, 0)

    pl.semaphore_wait(barrier, n_freq + 1)

    def coarse_copy(step):
        peer = lax.rem(col + step, n_freq)
        return pltpu.make_async_remote_copy(
            src_ref=outbox_coarse.at[peer],
            dst_ref=held_coarse.at[RIM_COARSE + col],
            send_sem=coarse_send.at[step],
            recv_sem=coarse_recv.at[step],
            device_id={"freq": peer},
        )

    def fine_copy(pair, step):
        peer = lax.rem(col + step, n_freq)
        return pltpu.make_async_remote_copy(
            src_ref=outbox.at[peer, pair],
            dst_ref=held.at[pair, 2 + col],
            send_sem=send_sem.at[pair, step],
            recv_sem=recv_sem.at[pair, step],
            device_id={"freq": peer},
        )

    def coarse_rim_copy(up):
        first, landing = (coarse_groups, 0) if up else (RIM_COARSE, RIM_COARSE + coarse_groups)
        return pltpu.make_async_remote_copy(
            src_ref=held_coarse.at[pl.ds(first, RIM_COARSE)],
            dst_ref=held_coarse.at[pl.ds(landing, RIM_COARSE)],
            send_sem=coarse_rim_send.at[int(up)],
            recv_sem=coarse_rim_recv.at[int(up)],
            device_id={"box": above if up else below},
        )

    def rim_copy(pair, up):
        first, landing = (n_freq, 0) if up else (2, 2 + n_freq)
        return pltpu.make_async_remote_copy(
            src_ref=held.at[pair, pl.ds(first, 2)],
            dst_ref=held.at[pair, pl.ds(landing, 2)],
            send_sem=rim_send.at[pair, int(up)],
            recv_sem=rim_recv.at[pair, int(up)],
            device_id={"box": above if up else below},
        )

    for step in order:
        coarse_copy(step).start()
    for pair in range(PAIRS):
        for step in order:
            fine_copy(pair, step).start()
    held_coarse[RIM_COARSE + col] = outbox_coarse[col]
    for pair in range(PAIRS):
        held[pair, 2 + col] = outbox[col, pair]
        held[pair, 14] = jnp.zeros((16, WIDE), jnp.bfloat16)
        held[pair, 15] = jnp.zeros((16, WIDE), jnp.bfloat16)
    for blank in range(2 * RIM_COARSE + coarse_groups, 16):
        held_coarse[blank] = jnp.zeros((16, LANES), jnp.bfloat16)

    fine_list = lists_fine_ref[...]
    fine_at = fine_list - (box * groups - RIM_FINE)
    fine_row = jnp.where(fine_list >= 0, (fine_at // 8) * 16 + fine_at % 8, -1000)
    coarse_list = lists_coarse_ref[...]
    coarse_at = coarse_list - (box * coarse_groups - RIM_COARSE)
    coarse_row = jnp.where(coarse_list >= 0, 192 + coarse_at, -1000)
    lane_fine = lax.broadcasted_iota(jnp.int32, (groups, WIDE), 1)
    lane_coarse = lax.broadcasted_iota(jnp.int32, (coarse_groups, WIDE), 1)
    no_rows = jnp.zeros((16 - coarse_groups, WIDE), jnp.float32)
    for k in range(slots):
        for odd in range(2):
            picks[odd, pl.ds(k * rows, groups)] = jnp.where(
                fine_row[:, k : k + 1] + 8 * odd == lane_fine, 1.0, 0.0
            ).astype(jnp.bfloat16)
            coarse_hit = jnp.where(coarse_row[:, k : k + 1] + 16 * odd == lane_coarse, 1.0, 0.0)
            picks[odd, pl.ds(k * rows + groups, 16)] = jnp.concatenate(
                [coarse_hit, no_rows], axis=0
            ).astype(jnp.bfloat16)

    lane_band = lax.broadcasted_iota(jnp.int32, (16, WIDE), 1) % BAND

    def widen(k, carry):
        table = [
            swap_blocks([table_ref[k, c, o].astype(jnp.float32) for o in range(8)]) for c in range(2)
        ]
        for g in range(BANDS):
            real, imag = table[0][g], table[1][g]
            full = jnp.concatenate(
                [
                    jnp.concatenate([real, imag], axis=1),
                    jnp.concatenate([-imag, real], axis=1),
                ],
                axis=0,
            ).astype(jnp.bfloat16)
            for f in range(BAND):
                weights[g, k, pl.ds(f * 16, 16)] = jnp.where(lane_band == f, full, jnp.zeros_like(full))
        return carry

    lax.fori_loop(0, slots, widen, 0)

    for step in order:
        coarse_copy(step).wait_recv()
    for up in (True, False):
        coarse_rim_copy(up).start()
    for up in (True, False):
        coarse_rim_copy(up).wait_recv()
    coarse_parts = [held_coarse[:, pl.ds(8 * c, 8)].astype(jnp.float32) for c in range(2)]
    coarse_bands = by_band(coarse_parts, permutation)
    for g in range(BANDS):
        held[g // 2, 12 + g % 2] = coarse_bands[16 * g : 16 * g + 16]

    def advance(turn, carry):
        @pl.when(turn < PAIRS)
        def _():
            for step in order:
                fine_copy(turn, step).wait_recv()
            for up in (True, False):
                rim_copy(turn, up).start()

        @pl.when(turn > 0)
        def _():
            pair = turn - 1
            for up in (True, False):
                rim_copy(pair, up).wait_recv()
            sources = held[pair].reshape(16 * 16, WIDE)
            for odd in range(2):
                gathered[...] = jnp.dot(
                    picks[odd], sources, preferred_element_type=jnp.float32
                ).astype(jnp.bfloat16)
                total = jnp.zeros((rows, WIDE), jnp.float32)
                for k in range(slots):
                    total = total + jnp.dot(
                        gathered[pl.ds(k * rows, rows)],
                        weights[2 * pair + odd, k],
                        preferred_element_type=jnp.float32,
                    )
                sums[2 * pair + odd] = total

        return carry

    lax.fori_loop(0, PAIRS + 1, advance, 0)

    def back(first, live, count, scale):
        keep = alive(first + lax.broadcasted_iota(jnp.int32, (8, 8, LANES), 0), count, live)
        result = []
        for c in range(2):
            planes = swap_blocks(
                [sums[g, pl.ds(first + scale[1], 8), pl.ds(c * LANES, LANES)] for g in range(BANDS)]
            )
            turned = jnp.swapaxes(jnp.stack(planes, axis=0), 0, 1)
            result.append(jnp.where(keep, scale[0] * turned, 0.0).astype(jnp.bfloat16))
        return result

    def finish(part, carry):
        first = pl.multiple_of(part * 8, 8)
        result = back(first, live_fine, groups, (1.0, 0))
        for c in range(2):
            out_fine_ref[pl.ds(first, 8), c] = result[c]
        return carry

    lax.fori_loop(0, groups // 8, finish, 0)
    result = back(0, live_coarse, coarse_groups, (0.5, groups))
    for c in range(2):
        out_coarse_ref[:, c] = result[c]

    for step in order:
        coarse_copy(step).wait_send()
        for pair in range(PAIRS):
            fine_copy(pair, step).wait_send()
    for up in (True, False):
        coarse_rim_copy(up).wait_send()
        for pair in range(PAIRS):
            rim_copy(pair, up).wait_send()


def per_device(n_box, n_freq, spectra_fine, spectra_coarse, kernel_table, lists_fine, lists_coarse, live_counts):
    groups, slots = lists_fine.shape
    coarse_groups = lists_coarse.shape[0]
    own = spectra_fine.shape[0]
    rows = groups + 16
    vmem = pl.BlockSpec(memory_space=pltpu.VMEM)
    dma = pltpu.SemaphoreType.DMA
    return pl.pallas_call(
        functools.partial(kernel, n_box, n_freq),
        out_shape=(
            jax.ShapeDtypeStruct((groups, 2, 8, LANES), jnp.bfloat16),
            jax.ShapeDtypeStruct((coarse_groups, 2, 8, LANES), jnp.bfloat16),
        ),
        in_specs=[pl.BlockSpec(memory_space=pltpu.SMEM)] + [vmem] * 5,
        out_specs=(vmem, vmem),
        scratch_shapes=[
            pltpu.VMEM((n_freq, PAIRS, 2 * own, WIDE), jnp.bfloat16),
            pltpu.VMEM((n_freq, 16, LANES), jnp.bfloat16),
            pltpu.VMEM((PAIRS, 16, 16, WIDE), jnp.bfloat16),
            pltpu.VMEM((16, 16, LANES), jnp.bfloat16),
            pltpu.VMEM((2, slots * rows, WIDE), jnp.bfloat16),
            pltpu.VMEM((BANDS, slots, WIDE, WIDE), jnp.bfloat16),
            pltpu.VMEM((slots * rows, WIDE), jnp.bfloat16),
            pltpu.VMEM((BANDS, rows, WIDE), jnp.float32),
            dma((PAIRS, n_freq)),
            dma((PAIRS, n_freq)),
            dma((PAIRS, 2)),
            dma((PAIRS, 2)),
            dma((n_freq,)),
            dma((n_freq,)),
            dma((2,)),
            dma((2,)),
        ],
        compiler_params=pltpu.CompilerParams(
            collective_id=0, has_side_effects=True, vmem_limit_bytes=56 * 1024 * 1024
        ),
    )(live_counts, spectra_fine, spectra_coarse, kernel_table, lists_fine, lists_coarse)


def solution(mesh):
    return jax.shard_map(
        functools.partial(per_device, mesh.shape["box"], mesh.shape["freq"]),
        mesh=mesh,
        in_specs=(
            P(("box", "freq"), None, None, None),
            P(("box", "freq"), None, None, None),
            P(None, None, None, None, "freq"),
            P("box", None),
            P("box", None),
            P("box", None),
        ),
        out_specs=(P("box", None, None, "freq"), P("box", None, None, "freq")),
        check_vma=False,
    )
```

```python
import functools

import jax
import jax.numpy as jnp
from jax import lax
from jax.experimental import pallas as pl
from jax.experimental.pallas import tpu as pltpu
from jax.sharding import PartitionSpec as P

RIM_FINE = 16
RIM_COARSE = 2
HALF = 8
LANES = 128
BAND = 16
BANDS = LANES // BAND
PAIRS = BANDS // 2
WIDE = 2 * 8 * BAND


def swap_blocks(planes):
    block = lax.broadcasted_iota(jnp.int32, planes[0].shape, 1) // BAND
    planes = list(planes)
    for step in (4, 2, 1):
        upper = (block & step) != 0
        for p in range(8):
            if p & step == 0:
                first, second = planes[p], planes[p + step]
                planes[p] = jnp.where(upper, pltpu.roll(second, BAND * step, 1), first)
                planes[p + step] = jnp.where(upper, second, pltpu.roll(first, LANES - BAND * step, 1))
    return planes


def interleave():
    row = lax.broadcasted_iota(jnp.int32, (WIDE, WIDE), 0)
    lane = lax.broadcasted_iota(jnp.int32, (WIDE, WIDE), 1)
    hit = (row // BAND == lane % BAND) & (row % BAND == lane // BAND)
    return jnp.where(hit, 1.0, 0.0).astype(jnp.bfloat16)


def by_band(parts, permutation):
    planes = []
    for part in parts:
        turned = jnp.swapaxes(part, 0, 1)
        planes.append(swap_blocks([turned[i] for i in range(8)]))
    stacked = jnp.concatenate(
        [jnp.concatenate([planes[0][g], planes[1][g]], axis=1) for g in range(BANDS)], axis=0
    ).astype(jnp.bfloat16)
    return jnp.dot(stacked, permutation, preferred_element_type=jnp.float32).astype(jnp.bfloat16)


def alive(place, count, live):
    lower = live // 2
    return (place < lower) | (place >= count - (live - lower))


def kernel(
    n_box,
    n_freq,
    live_ref,
    fine_ref,
    coarse_ref,
    table_ref,
    lists_fine_ref,
    lists_coarse_ref,
    out_fine_ref,
    out_coarse_ref,
    outbox,
    outbox_coarse,
    held,
    held_coarse,
    picks,
    weights,
    gathered,
    sums,
    send_sem,
    recv_sem,
    rim_send,
    rim_recv,
    coarse_send,
    coarse_recv,
    coarse_rim_send,
    coarse_rim_recv,
    far_send,
    far_recv,
):
    box = lax.axis_index("box")
    col = lax.axis_index("freq")
    above = lax.rem(box + 1, n_box)
    below = lax.rem(box + n_box - 1, n_box)
    slots = table_ref.shape[0]
    groups = lists_fine_ref.shape[1]
    coarse_groups = lists_coarse_ref.shape[1]
    own = fine_ref.shape[0]
    rows = groups + 16
    live_fine = live_ref[0, 0]
    live_coarse = live_ref[0, 1]
    order = (4, 3, 5, 2, 6, 1, 7)

    has_above, has_below = box < n_box - 1, box > 0
    far_above = has_above & (lax.rem(box, HALF) == HALF - 1)
    far_below = has_below & (lax.rem(box, HALF) == 0)
    near_above = has_above & (lax.rem(box, HALF) != HALF - 1)
    near_below = has_below & (lax.rem(box, HALF) != 0)
    gives_above = far_above & (col >= n_freq - 2)
    gives_below = far_below & (col < 2)

    barrier = pltpu.get_barrier_semaphore()
    for step in range(1, n_freq):
        pl.semaphore_signal(barrier, inc=1, device_id={"freq": lax.rem(col + step, n_freq)})
    for near, other in ((near_above, above), (near_below, below)):

        @pl.when(near)
        def _():
            pl.semaphore_signal(barrier, inc=1, device_id={"box": other})

    for far, other, first in ((far_above, above, 0), (far_below, below, n_freq - 2)):

        @pl.when(far)
        def _():
            for i in range(2):
                pl.semaphore_signal(barrier, inc=1, device_id={"box": other, "freq": first + i})

    ready = (
        n_freq
        - 1
        + near_above.astype(jnp.int32)
        + near_below.astype(jnp.int32)
        + n_freq * gives_above.astype(jnp.int32)
        + n_freq * gives_below.astype(jnp.int32)
    )

    permutation = interleave()

    place = col * own + lax.broadcasted_iota(jnp.int32, (own, 8, LANES), 0)
    fine_alive = alive(place, groups, live_fine)
    coarse_alive = alive(jnp.full((16, LANES), col, jnp.int32), coarse_groups, live_coarse)

    def cut(j, carry):
        lanes = pl.ds(pl.multiple_of(j * LANES, LANES), LANES)
        parts = [
            jnp.where(fine_alive, fine_ref[:, c, :, lanes].astype(jnp.float32), 0.0) for c in range(2)
        ]
        outbox[j] = by_band(parts, permutation).reshape(PAIRS, 2 * own, WIDE)
        both = jnp.concatenate(
            [coarse_ref[0, c, :, lanes].astype(jnp.float32) for c in range(2)], axis=0
        )
        outbox_coarse[j] = jnp.where(coarse_alive, both, 0.0).astype(jnp.bfloat16)
        return carry

    lax.fori_loop(0, n_freq, cut, 0, unroll=True)

    pl.semaphore_wait(barrier, ready)

    def coarse_copy(step):
        peer = lax.rem(col + step, n_freq)
        return pltpu.make_async_remote_copy(
            src_ref=outbox_coarse.at[peer],
            dst_ref=held_coarse.at[RIM_COARSE + col],
            send_sem=coarse_send.at[step],
            recv_sem=coarse_recv.at[step],
            device_id={"freq": peer},
        )

    def fine_copy(pair, step):
        peer = lax.rem(col + step, n_freq)
        return pltpu.make_async_remote_copy(
            src_ref=outbox.at[peer, pair],
            dst_ref=held.at[pair, 2 + col],
            send_sem=send_sem.at[pair, step],
            recv_sem=recv_sem.at[pair, step],
            device_id={"freq": peer},
        )

    def coarse_rim_copy(up):
        first, landing = (coarse_groups, 0) if up else (RIM_COARSE, RIM_COARSE + coarse_groups)
        return pltpu.make_async_remote_copy(
            src_ref=held_coarse.at[pl.ds(first, RIM_COARSE)],
            dst_ref=held_coarse.at[pl.ds(landing, RIM_COARSE)],
            send_sem=coarse_rim_send.at[int(up)],
            recv_sem=coarse_rim_recv.at[int(up)],
            device_id={"box": above if up else below},
        )

    def rim_copy(pair, up):
        first, landing = (n_freq, 0) if up else (2, 2 + n_freq)
        return pltpu.make_async_remote_copy(
            src_ref=held.at[pair, pl.ds(first, 2)],
            dst_ref=held.at[pair, pl.ds(landing, 2)],
            send_sem=rim_send.at[pair, int(up)],
            recv_sem=rim_recv.at[pair, int(up)],
            device_id={"box": above if up else below},
        )

    def far_copies(up, pair):
        if up:
            other, landing, index = above, col - (n_freq - 2), lax.rem(col, 2)
        else:
            other, landing, index = below, n_freq + 2 + col, lax.rem(col, 2)
        copies = []
        for j in range(n_freq):
            if pair is None:
                source, target = outbox_coarse.at[j], held_coarse.at[landing]
            else:
                source, target = outbox.at[j, pair], held.at[pair, landing]
            lot = PAIRS if pair is None else pair
            copies.append(
                pltpu.make_async_remote_copy(
                    src_ref=source,
                    dst_ref=target,
                    send_sem=far_send.at[int(up), lot, j],
                    recv_sem=far_recv.at[int(up), lot, index],
                    device_id={"box": other, "freq": j},
                )
            )
        return copies

    def far_wait(up, pair):
        for i in range(2):
            landing = i if up else n_freq + 2 + i
            if pair is None:
                here = held_coarse.at[landing]
            else:
                here = held.at[pair, landing]
            lot = PAIRS if pair is None else pair
            pltpu.make_async_copy(here, here, far_recv.at[int(up), lot, i]).wait()

    def start_far(pair):
        for up, gives in ((True, gives_above), (False, gives_below)):

            @pl.when(gives)
            def _():
                for copy in far_copies(up, pair):
                    copy.start()

    start_far(None)
    for step in order:
        coarse_copy(step).start()
    for pair in range(PAIRS):
        start_far(pair)
        for step in order:
            fine_copy(pair, step).start()
    held_coarse[RIM_COARSE + col] = outbox_coarse[col]
    for pair in range(PAIRS):
        held[pair, 2 + col] = outbox[col, pair]
        held[pair, 14] = jnp.zeros((16, WIDE), jnp.bfloat16)
        held[pair, 15] = jnp.zeros((16, WIDE), jnp.bfloat16)

    @pl.when(jnp.logical_not(has_below))
    def _():
        for pair in range(PAIRS):
            for i in range(2):
                held[pair, i] = jnp.zeros((16, WIDE), jnp.bfloat16)
        for i in range(2):
            held_coarse[i] = jnp.zeros((16, LANES), jnp.bfloat16)

    @pl.when(jnp.logical_not(has_above))
    def _():
        for pair in range(PAIRS):
            for i in range(2):
                held[pair, n_freq + 2 + i] = jnp.zeros((16, WIDE), jnp.bfloat16)
        for i in range(2):
            held_coarse[n_freq + 2 + i] = jnp.zeros((16, LANES), jnp.bfloat16)

    for blank in range(2 * RIM_COARSE + coarse_groups, 16):
        held_coarse[blank] = jnp.zeros((16, LANES), jnp.bfloat16)

    fine_list = jnp.transpose(lists_fine_ref[...])
    fine_at = fine_list - (box * groups - RIM_FINE)
    fine_row = jnp.where(fine_list >= 0, (fine_at // 8) * 16 + fine_at % 8, -1000)
    coarse_list = jnp.transpose(lists_coarse_ref[...])
    coarse_at = coarse_list - (box * coarse_groups - RIM_COARSE)
    coarse_row = jnp.where(coarse_list >= 0, 192 + coarse_at, -1000)
    lane_fine = lax.broadcasted_iota(jnp.int32, (groups, WIDE), 1)
    lane_coarse = lax.broadcasted_iota(jnp.int32, (coarse_groups, WIDE), 1)
    no_rows = jnp.zeros((16 - coarse_groups, WIDE), jnp.float32)
    for k in range(slots):
        for odd in range(2):
            picks[odd, pl.ds(k * rows, groups)] = jnp.where(
                fine_row[:, k : k + 1] + 8 * odd == lane_fine, 1.0, 0.0
            ).astype(jnp.bfloat16)
            coarse_hit = jnp.where(coarse_row[:, k : k + 1] + 16 * odd == lane_coarse, 1.0, 0.0)
            picks[odd, pl.ds(k * rows + groups, 16)] = jnp.concatenate(
                [coarse_hit, no_rows], axis=0
            ).astype(jnp.bfloat16)

    lane_band = lax.broadcasted_iota(jnp.int32, (16, WIDE), 1) % BAND

    def widen(k, carry):
        table = [
            swap_blocks([table_ref[k, c, o].astype(jnp.float32) for o in range(8)]) for c in range(2)
        ]
        for g in range(BANDS):
            real, imag = table[0][g], table[1][g]
            full = jnp.concatenate(
                [
                    jnp.concatenate([real, imag], axis=1),
                    jnp.concatenate([-imag, real], axis=1),
                ],
                axis=0,
            ).astype(jnp.bfloat16)
            for f in range(BAND):
                weights[g, k, pl.ds(f * 16, 16)] = jnp.where(lane_band == f, full, jnp.zeros_like(full))
        return carry

    lax.fori_loop(0, slots, widen, 0, unroll=2)

    def rim_start(copy):
        for up, near in ((True, near_above), (False, near_below)):

            @pl.when(near)
            def _():
                copy(up).start()

    def rim_wait(copy, pair):
        for up, near, far in ((True, near_below, far_below), (False, near_above, far_above)):

            @pl.when(near)
            def _():
                copy(up).wait_recv()

            @pl.when(far)
            def _():
                far_wait(up, pair)

    def arrive(pair):
        for step in order:
            fine_copy(pair, step).wait_recv()
        rim_start(lambda up: rim_copy(pair, up))

    for step in order:
        coarse_copy(step).wait_recv()
    rim_start(coarse_rim_copy)
    arrive(0)
    rim_wait(coarse_rim_copy, None)
    coarse_parts = [held_coarse[:, pl.ds(8 * c, 8)].astype(jnp.float32) for c in range(2)]
    coarse_bands = by_band(coarse_parts, permutation)
    for g in range(BANDS):
        held[g // 2, 12 + g % 2] = coarse_bands[16 * g : 16 * g + 16]

    def advance(pair, carry):
        @pl.when(pair < PAIRS - 1)
        def _():
            arrive(pair + 1)

        rim_wait(lambda up: rim_copy(pair, up), pair)
        sources = held[pair].reshape(16 * 16, WIDE)
        for odd in range(2):
            gathered[...] = jnp.dot(
                picks[odd], sources, preferred_element_type=jnp.float32
            ).astype(jnp.bfloat16)
            total = jnp.zeros((rows, WIDE), jnp.float32)
            for k in range(slots):
                total = total + jnp.dot(
                    gathered[pl.ds(k * rows, rows)],
                    weights[2 * pair + odd, k],
                    preferred_element_type=jnp.float32,
                )
            sums[2 * pair + odd] = total
        return carry

    lax.fori_loop(0, PAIRS, advance, 0)

    def back(first, live, count, scale):
        keep = alive(first + lax.broadcasted_iota(jnp.int32, (8, 8, LANES), 0), count, live)
        result = []
        for c in range(2):
            planes = swap_blocks(
                [sums[g, pl.ds(first + scale[1], 8), pl.ds(c * LANES, LANES)] for g in range(BANDS)]
            )
            turned = jnp.swapaxes(jnp.stack(planes, axis=0), 0, 1)
            result.append(jnp.where(keep, scale[0] * turned, 0.0).astype(jnp.bfloat16))
        return result

    def finish(part, carry):
        first = pl.multiple_of(part * 8, 8)
        result = back(first, live_fine, groups, (1.0, 0))
        for c in range(2):
            out_fine_ref[pl.ds(first, 8), c] = result[c]
        return carry

    lax.fori_loop(0, groups // 8, finish, 0, unroll=True)
    result = back(0, live_coarse, coarse_groups, (0.5, groups))
    for c in range(2):
        out_coarse_ref[:, c] = result[c]

    for step in order:
        coarse_copy(step).wait_send()
        for pair in range(PAIRS):
            fine_copy(pair, step).wait_send()
    for up, near, gives in ((True, near_above, gives_above), (False, near_below, gives_below)):

        @pl.when(near)
        def _():
            coarse_rim_copy(up).wait_send()
            for pair in range(PAIRS):
                rim_copy(pair, up).wait_send()

        @pl.when(gives)
        def _():
            for pair in (None, *range(PAIRS)):
                for copy in far_copies(up, pair):
                    copy.wait_send()


def per_device(n_box, n_freq, spectra_fine, spectra_coarse, kernel_table, lists_fine, lists_coarse, live_counts):
    groups, slots = lists_fine.shape
    coarse_groups = lists_coarse.shape[0]
    own = spectra_fine.shape[0]
    rows = groups + 16
    vmem = pl.BlockSpec(memory_space=pltpu.VMEM)
    dma = pltpu.SemaphoreType.DMA
    return pl.pallas_call(
        functools.partial(kernel, n_box, n_freq),
        out_shape=(
            jax.ShapeDtypeStruct((groups, 2, 8, LANES), jnp.bfloat16),
            jax.ShapeDtypeStruct((coarse_groups, 2, 8, LANES), jnp.bfloat16),
        ),
        in_specs=[pl.BlockSpec(memory_space=pltpu.SMEM)] + [vmem] * 5,
        out_specs=(vmem, vmem),
        scratch_shapes=[
            pltpu.VMEM((n_freq, PAIRS, 2 * own, WIDE), jnp.bfloat16),
            pltpu.VMEM((n_freq, 16, LANES), jnp.bfloat16),
            pltpu.VMEM((PAIRS, 16, 16, WIDE), jnp.bfloat16),
            pltpu.VMEM((16, 16, LANES), jnp.bfloat16),
            pltpu.VMEM((2, slots * rows, WIDE), jnp.bfloat16),
            pltpu.VMEM((BANDS, slots, WIDE, WIDE), jnp.bfloat16),
            pltpu.VMEM((slots * rows, WIDE), jnp.bfloat16),
            pltpu.VMEM((BANDS, rows, WIDE), jnp.float32),
            dma((PAIRS, n_freq)),
            dma((PAIRS, n_freq)),
            dma((PAIRS, 2)),
            dma((PAIRS, 2)),
            dma((n_freq,)),
            dma((n_freq,)),
            dma((2,)),
            dma((2,)),
            dma((2, PAIRS + 1, n_freq)),
            dma((2, PAIRS + 1, 2)),
        ],
        compiler_params=pltpu.CompilerParams(
            collective_id=0, has_side_effects=True, vmem_limit_bytes=56 * 1024 * 1024
        ),
    )(live_counts, spectra_fine, spectra_coarse, kernel_table, lists_fine.T, lists_coarse.T)


def solution(mesh):
    return jax.shard_map(
        functools.partial(per_device, mesh.shape["box"], mesh.shape["freq"]),
        mesh=mesh,
        in_specs=(
            P(("box", "freq"), None, None, None),
            P(("box", "freq"), None, None, None),
            P(None, None, None, None, "freq"),
            P("box", None),
            P("box", None),
            P("box", None),
        ),
        out_specs=(P("box", None, None, "freq"), P("box", None, None, "freq")),
        check_vma=False,
    )
```

```python
import functools

import jax
import jax.numpy as jnp
from jax import lax
from jax.experimental import pallas as pl
from jax.experimental.pallas import tpu as pltpu
from jax.sharding import PartitionSpec as P

RIM_FINE = 16
RIM_COARSE = 2
HALF = 8
LANES = 128
BAND = 16
BANDS = LANES // BAND
PAIRS = BANDS // 2
WIDE = 2 * 8 * BAND


def swap_blocks(planes):
    block = lax.broadcasted_iota(jnp.int32, planes[0].shape, 1) // BAND
    planes = list(planes)
    for step in (4, 2, 1):
        upper = (block & step) != 0
        for p in range(8):
            if p & step == 0:
                first, second = planes[p], planes[p + step]
                planes[p] = jnp.where(upper, pltpu.roll(second, BAND * step, 1), first)
                planes[p + step] = jnp.where(upper, second, pltpu.roll(first, LANES - BAND * step, 1))
    return planes


def interleave():
    row = lax.broadcasted_iota(jnp.int32, (WIDE, WIDE), 0)
    lane = lax.broadcasted_iota(jnp.int32, (WIDE, WIDE), 1)
    hit = (row // BAND == lane % BAND) & (row % BAND == lane // BAND)
    return jnp.where(hit, 1.0, 0.0).astype(jnp.bfloat16)


def by_band(parts, permutation):
    planes = []
    for part in parts:
        turned = jnp.swapaxes(part, 0, 1)
        planes.append(swap_blocks([turned[i] for i in range(8)]))
    stacked = jnp.concatenate(
        [jnp.concatenate([planes[0][g], planes[1][g]], axis=1) for g in range(BANDS)], axis=0
    ).astype(jnp.bfloat16)
    return jnp.dot(stacked, permutation, preferred_element_type=jnp.float32).astype(jnp.bfloat16)


def alive(place, count, live):
    lower = live // 2
    return (place < lower) | (place >= count - (live - lower))


def kernel(
    n_box,
    n_freq,
    live_ref,
    fine_ref,
    coarse_ref,
    table_ref,
    lists_fine_ref,
    lists_coarse_ref,
    out_fine_ref,
    out_coarse_ref,
    outbox,
    outbox_coarse,
    held,
    held_coarse,
    picks,
    weights,
    gathered,
    sums,
    send_sem,
    recv_sem,
    rim_send,
    rim_recv,
    coarse_send,
    coarse_recv,
    coarse_rim_send,
    coarse_rim_recv,
    far_send,
    far_recv,
    ready_sem,
    far_ready,
):
    box = lax.axis_index("box")
    col = lax.axis_index("freq")
    above = lax.rem(box + 1, n_box)
    below = lax.rem(box + n_box - 1, n_box)
    slots = table_ref.shape[0]
    groups = lists_fine_ref.shape[1]
    coarse_groups = lists_coarse_ref.shape[1]
    own = fine_ref.shape[0]
    rows = groups + 16
    live_fine = live_ref[0, 0]
    live_coarse = live_ref[0, 1]
    steps = tuple(range(1, n_freq))

    has_above, has_below = box < n_box - 1, box > 0
    far_above = has_above & (lax.rem(box, HALF) == HALF - 1)
    far_below = has_below & (lax.rem(box, HALF) == 0)
    near_above = has_above & (lax.rem(box, HALF) != HALF - 1)
    near_below = has_below & (lax.rem(box, HALF) != 0)
    gives_above = far_above & (col >= n_freq - 2)
    gives_below = far_below & (col < 2)

    first, last = col == 0, col == n_freq - 1
    early = lax.rem(box // HALF, 2) == 0

    def signal(semaphore, **device):
        pl.semaphore_signal(semaphore, inc=1, device_id=device)

    barrier = pltpu.get_barrier_semaphore()
    for near, other in ((near_above, above), (near_below, below)):

        @pl.when(near)
        def _():
            signal(barrier, box=other)

    @pl.when(gives_below)
    def _():
        signal(barrier, box=below, freq=n_freq - 1)

    ready = (
        jnp.where(first, 0, 1)
        + near_above.astype(jnp.int32)
        + near_below.astype(jnp.int32)
        + jnp.where(far_above & last, 2, 0)
    )

    permutation = interleave()

    place = col * own + lax.broadcasted_iota(jnp.int32, (own, 8, LANES), 0)
    fine_alive = alive(place, groups, live_fine)
    coarse_alive = alive(jnp.full((16, LANES), col, jnp.int32), coarse_groups, live_coarse)

    def cut(j, carry):
        lanes = pl.ds(pl.multiple_of(j * LANES, LANES), LANES)
        parts = [
            jnp.where(fine_alive, fine_ref[:, c, :, lanes].astype(jnp.float32), 0.0) for c in range(2)
        ]
        outbox[j] = by_band(parts, permutation).reshape(PAIRS, 2 * own, WIDE)
        both = jnp.concatenate(
            [coarse_ref[0, c, :, lanes].astype(jnp.float32) for c in range(2)], axis=0
        )
        outbox_coarse[j] = jnp.where(coarse_alive, both, 0.0).astype(jnp.bfloat16)
        return carry

    lax.fori_loop(0, n_freq, cut, 0, unroll=True)

    pl.semaphore_wait(barrier, ready)

    @pl.when(jnp.logical_not(last))
    def _():
        signal(barrier, freq=col + 1)

    for step in steps:

        @pl.when(col >= step)
        def _():
            signal(ready_sem.at[step], freq=col - step)

    @pl.when(far_above & last)
    def _():
        for i in range(2):
            signal(far_ready.at[0], box=above, freq=i)

    def coarse_copy(step):
        peer = lax.rem(col + step, n_freq)
        return pltpu.make_async_remote_copy(
            src_ref=outbox_coarse.at[peer],
            dst_ref=held_coarse.at[RIM_COARSE + col],
            send_sem=coarse_send.at[step],
            recv_sem=coarse_recv.at[step],
            device_id={"freq": peer},
        )

    def fine_copy(pair, step):
        peer = lax.rem(col + step, n_freq)
        return pltpu.make_async_remote_copy(
            src_ref=outbox.at[peer, pair],
            dst_ref=held.at[pair, 2 + col],
            send_sem=send_sem.at[pair, step],
            recv_sem=recv_sem.at[pair, step],
            device_id={"freq": peer},
        )

    def coarse_rim_copy(up):
        first, landing = (coarse_groups, 0) if up else (RIM_COARSE, RIM_COARSE + coarse_groups)
        return pltpu.make_async_remote_copy(
            src_ref=held_coarse.at[pl.ds(first, RIM_COARSE)],
            dst_ref=held_coarse.at[pl.ds(landing, RIM_COARSE)],
            send_sem=coarse_rim_send.at[int(up)],
            recv_sem=coarse_rim_recv.at[int(up)],
            device_id={"box": above if up else below},
        )

    def rim_copy(pair, up):
        first, landing = (n_freq, 0) if up else (2, 2 + n_freq)
        return pltpu.make_async_remote_copy(
            src_ref=held.at[pair, pl.ds(first, 2)],
            dst_ref=held.at[pair, pl.ds(landing, 2)],
            send_sem=rim_send.at[pair, int(up)],
            recv_sem=rim_recv.at[pair, int(up)],
            device_id={"box": above if up else below},
        )

    def far_copies(up, pair):
        if up:
            other, landing, index = above, col - (n_freq - 2), lax.rem(col, 2)
        else:
            other, landing, index = below, n_freq + 2 + col, lax.rem(col, 2)
        copies = []
        for j in range(n_freq):
            if pair is None:
                source, target = outbox_coarse.at[j], held_coarse.at[landing]
            else:
                source, target = outbox.at[j, pair], held.at[pair, landing]
            lot = PAIRS if pair is None else pair
            copies.append(
                pltpu.make_async_remote_copy(
                    src_ref=source,
                    dst_ref=target,
                    send_sem=far_send.at[int(up), lot, j],
                    recv_sem=far_recv.at[int(up), lot, index],
                    device_id={"box": other, "freq": j},
                )
            )
        return copies

    def far_wait(up, pair):
        for i in range(2):
            landing = i if up else n_freq + 2 + i
            if pair is None:
                here = held_coarse.at[landing]
            else:
                here = held.at[pair, landing]
            lot = PAIRS if pair is None else pair
            pltpu.make_async_copy(here, here, far_recv.at[int(up), lot, i]).wait()

    for pair in (None, *range(PAIRS)):
        for step in steps:

            @pl.when(col + step >= n_freq)
            def _():
                (coarse_copy(step) if pair is None else fine_copy(pair, step)).start()

    def send_on():
        for step in steps:

            @pl.when(col + step < n_freq)
            def _():
                pl.semaphore_wait(ready_sem.at[step], 1)
                coarse_copy(step).start()
                for pair in range(PAIRS):
                    fine_copy(pair, step).start()

        @pl.when(gives_below)
        def _():
            pl.semaphore_wait(far_ready.at[0], 1)

        @pl.when(far_below & first)
        def _():
            signal(far_ready.at[1], box=below, freq=n_freq - 1)

        @pl.when(far_above & last)
        def _():
            pl.semaphore_wait(far_ready.at[1], 1)
            signal(far_ready.at[2], freq=n_freq - 2)

        @pl.when(far_above & (col == n_freq - 2))
        def _():
            pl.semaphore_wait(far_ready.at[2], 1)

        for up, gives in ((True, gives_above), (False, gives_below)):

            @pl.when(gives)
            def _():
                for pair in (None, *range(PAIRS)):
                    for copy in far_copies(up, pair):
                        copy.start()

    held_coarse[RIM_COARSE + col] = outbox_coarse[col]
    for pair in range(PAIRS):
        held[pair, 2 + col] = outbox[col, pair]
        held[pair, 14] = jnp.zeros((16, WIDE), jnp.bfloat16)
        held[pair, 15] = jnp.zeros((16, WIDE), jnp.bfloat16)

    @pl.when(jnp.logical_not(has_below))
    def _():
        for pair in range(PAIRS):
            for i in range(2):
                held[pair, i] = jnp.zeros((16, WIDE), jnp.bfloat16)
        for i in range(2):
            held_coarse[i] = jnp.zeros((16, LANES), jnp.bfloat16)

    @pl.when(jnp.logical_not(has_above))
    def _():
        for pair in range(PAIRS):
            for i in range(2):
                held[pair, n_freq + 2 + i] = jnp.zeros((16, WIDE), jnp.bfloat16)
        for i in range(2):
            held_coarse[n_freq + 2 + i] = jnp.zeros((16, LANES), jnp.bfloat16)

    for blank in range(2 * RIM_COARSE + coarse_groups, 16):
        held_coarse[blank] = jnp.zeros((16, LANES), jnp.bfloat16)

    def prepare():
        fine_list = jnp.transpose(lists_fine_ref[...])
        fine_at = fine_list - (box * groups - RIM_FINE)
        fine_row = jnp.where(fine_list >= 0, (fine_at // 8) * 16 + fine_at % 8, -1000)
        coarse_list = jnp.transpose(lists_coarse_ref[...])
        coarse_at = coarse_list - (box * coarse_groups - RIM_COARSE)
        coarse_row = jnp.where(coarse_list >= 0, 192 + coarse_at, -1000)
        lane_fine = lax.broadcasted_iota(jnp.int32, (groups, WIDE), 1)
        lane_coarse = lax.broadcasted_iota(jnp.int32, (coarse_groups, WIDE), 1)
        no_rows = jnp.zeros((16 - coarse_groups, WIDE), jnp.float32)
        for k in range(slots):
            for odd in range(2):
                picks[odd, pl.ds(k * rows, groups)] = jnp.where(
                    fine_row[:, k : k + 1] + 8 * odd == lane_fine, 1.0, 0.0
                ).astype(jnp.bfloat16)
                coarse_hit = jnp.where(coarse_row[:, k : k + 1] + 16 * odd == lane_coarse, 1.0, 0.0)
                picks[odd, pl.ds(k * rows + groups, 16)] = jnp.concatenate(
                    [coarse_hit, no_rows], axis=0
                ).astype(jnp.bfloat16)

        lane_band = lax.broadcasted_iota(jnp.int32, (16, WIDE), 1) % BAND

        def widen(k, carry):
            table = [
                swap_blocks([table_ref[k, c, o].astype(jnp.float32) for o in range(8)]) for c in range(2)
            ]
            for g in range(BANDS):
                real, imag = table[0][g], table[1][g]
                full = jnp.concatenate(
                    [
                        jnp.concatenate([real, imag], axis=1),
                        jnp.concatenate([-imag, real], axis=1),
                    ],
                    axis=0,
                ).astype(jnp.bfloat16)
                for f in range(BAND):
                    weights[g, k, pl.ds(f * 16, 16)] = jnp.where(lane_band == f, full, jnp.zeros_like(full))
            return carry

        lax.fori_loop(0, slots, widen, 0, unroll=2)

    def middle(turn, carry):
        local = (turn == 0) == early

        @pl.when(local)
        def _():
            prepare()

        @pl.when(jnp.logical_not(local))
        def _():
            send_on()

        return carry

    lax.fori_loop(0, 2, middle, 0)

    def rim_start(copy):
        for up, near in ((True, near_above), (False, near_below)):

            @pl.when(near)
            def _():
                copy(up).start()

    def rim_wait(copy, pair):
        for up, near, far in ((True, near_below, far_below), (False, near_above, far_above)):

            @pl.when(near)
            def _():
                copy(up).wait_recv()

            @pl.when(far)
            def _():
                far_wait(up, pair)

    def arrive(pair):
        for step in steps:
            fine_copy(pair, step).wait_recv()
        rim_start(lambda up: rim_copy(pair, up))

    for step in steps:
        coarse_copy(step).wait_recv()
    rim_start(coarse_rim_copy)
    arrive(0)
    rim_wait(coarse_rim_copy, None)
    coarse_parts = [held_coarse[:, pl.ds(8 * c, 8)].astype(jnp.float32) for c in range(2)]
    coarse_bands = by_band(coarse_parts, permutation)
    for g in range(BANDS):
        held[g // 2, 12 + g % 2] = coarse_bands[16 * g : 16 * g + 16]

    def advance(pair, carry):
        @pl.when(pair < PAIRS - 1)
        def _():
            arrive(pair + 1)

        rim_wait(lambda up: rim_copy(pair, up), pair)
        sources = held[pair].reshape(16 * 16, WIDE)
        for odd in range(2):
            gathered[...] = jnp.dot(
                picks[odd], sources, preferred_element_type=jnp.float32
            ).astype(jnp.bfloat16)
            total = jnp.zeros((rows, WIDE), jnp.float32)
            for k in range(slots):
                total = total + jnp.dot(
                    gathered[pl.ds(k * rows, rows)],
                    weights[2 * pair + odd, k],
                    preferred_element_type=jnp.float32,
                )
            sums[2 * pair + odd] = total
        return carry

    lax.fori_loop(0, PAIRS, advance, 0)

    def back(first, live, count, scale):
        keep = alive(first + lax.broadcasted_iota(jnp.int32, (8, 8, LANES), 0), count, live)
        result = []
        for c in range(2):
            planes = swap_blocks(
                [sums[g, pl.ds(first + scale[1], 8), pl.ds(c * LANES, LANES)] for g in range(BANDS)]
            )
            turned = jnp.swapaxes(jnp.stack(planes, axis=0), 0, 1)
            result.append(jnp.where(keep, scale[0] * turned, 0.0).astype(jnp.bfloat16))
        return result

    def finish(part, carry):
        first = pl.multiple_of(part * 8, 8)
        result = back(first, live_fine, groups, (1.0, 0))
        for c in range(2):
            out_fine_ref[pl.ds(first, 8), c] = result[c]
        return carry

    lax.fori_loop(0, groups // 8, finish, 0, unroll=True)
    result = back(0, live_coarse, coarse_groups, (0.5, groups))
    for c in range(2):
        out_coarse_ref[:, c] = result[c]

    for step in steps:
        coarse_copy(step).wait_send()
        for pair in range(PAIRS):
            fine_copy(pair, step).wait_send()
    for up, near, gives in ((True, near_above, gives_above), (False, near_below, gives_below)):

        @pl.when(near)
        def _():
            coarse_rim_copy(up).wait_send()
            for pair in range(PAIRS):
                rim_copy(pair, up).wait_send()

        @pl.when(gives)
        def _():
            for pair in (None, *range(PAIRS)):
                for copy in far_copies(up, pair):
                    copy.wait_send()


def per_device(n_box, n_freq, spectra_fine, spectra_coarse, kernel_table, lists_fine, lists_coarse, live_counts):
    groups, slots = lists_fine.shape
    coarse_groups = lists_coarse.shape[0]
    own = spectra_fine.shape[0]
    rows = groups + 16
    vmem = pl.BlockSpec(memory_space=pltpu.VMEM)
    dma = pltpu.SemaphoreType.DMA
    return pl.pallas_call(
        functools.partial(kernel, n_box, n_freq),
        out_shape=(
            jax.ShapeDtypeStruct((groups, 2, 8, LANES), jnp.bfloat16),
            jax.ShapeDtypeStruct((coarse_groups, 2, 8, LANES), jnp.bfloat16),
        ),
        in_specs=[pl.BlockSpec(memory_space=pltpu.SMEM)] + [vmem] * 5,
        out_specs=(vmem, vmem),
        scratch_shapes=[
            pltpu.VMEM((n_freq, PAIRS, 2 * own, WIDE), jnp.bfloat16),
            pltpu.VMEM((n_freq, 16, LANES), jnp.bfloat16),
            pltpu.VMEM((PAIRS, 16, 16, WIDE), jnp.bfloat16),
            pltpu.VMEM((16, 16, LANES), jnp.bfloat16),
            pltpu.VMEM((2, slots * rows, WIDE), jnp.bfloat16),
            pltpu.VMEM((BANDS, slots, WIDE, WIDE), jnp.bfloat16),
            pltpu.VMEM((slots * rows, WIDE), jnp.bfloat16),
            pltpu.VMEM((BANDS, rows, WIDE), jnp.float32),
            dma((PAIRS, n_freq)),
            dma((PAIRS, n_freq)),
            dma((PAIRS, 2)),
            dma((PAIRS, 2)),
            dma((n_freq,)),
            dma((n_freq,)),
            dma((2,)),
            dma((2,)),
            dma((2, PAIRS + 1, n_freq)),
            dma((2, PAIRS + 1, 2)),
            pltpu.SemaphoreType.REGULAR((n_freq,)),
            pltpu.SemaphoreType.REGULAR((3,)),
        ],
        compiler_params=pltpu.CompilerParams(
            collective_id=0, has_side_effects=True, vmem_limit_bytes=56 * 1024 * 1024
        ),
    )(live_counts, spectra_fine, spectra_coarse, kernel_table, lists_fine.T, lists_coarse.T)


def solution(mesh):
    return jax.shard_map(
        functools.partial(per_device, mesh.shape["box"], mesh.shape["freq"]),
        mesh=mesh,
        in_specs=(
            P(("box", "freq"), None, None, None),
            P(("box", "freq"), None, None, None),
            P(None, None, None, None, "freq"),
            P("box", None),
            P("box", None),
            P("box", None),
        ),
        out_specs=(P("box", None, None, "freq"), P("box", None, None, "freq")),
        check_vma=False,
    )
```

```python
import functools

import jax
import jax.numpy as jnp
from jax import lax
from jax.experimental import pallas as pl
from jax.experimental.pallas import tpu as pltpu
from jax.sharding import PartitionSpec as P

RIM_FINE = 16
RIM_COARSE = 2
HALF = 8
LANES = 128
BAND = 16
BANDS = LANES // BAND
PAIRS = BANDS // 2
WIDE = 2 * 8 * BAND


def swap_blocks(planes):
    block = lax.broadcasted_iota(jnp.int32, planes[0].shape, 1) // BAND
    planes = list(planes)
    for step in (4, 2, 1):
        upper = (block & step) != 0
        for p in range(8):
            if p & step == 0:
                first, second = planes[p], planes[p + step]
                planes[p] = jnp.where(upper, pltpu.roll(second, BAND * step, 1), first)
                planes[p + step] = jnp.where(upper, second, pltpu.roll(first, LANES - BAND * step, 1))
    return planes


def interleave():
    row = lax.broadcasted_iota(jnp.int32, (WIDE, WIDE), 0)
    lane = lax.broadcasted_iota(jnp.int32, (WIDE, WIDE), 1)
    hit = (row // BAND == lane % BAND) & (row % BAND == lane // BAND)
    return jnp.where(hit, 1.0, 0.0).astype(jnp.bfloat16)


def by_band(parts, permutation):
    planes = []
    for part in parts:
        turned = jnp.swapaxes(part, 0, 1)
        planes.append(swap_blocks([turned[i] for i in range(8)]))
    stacked = jnp.concatenate(
        [jnp.concatenate([planes[0][g], planes[1][g]], axis=1) for g in range(BANDS)], axis=0
    ).astype(jnp.bfloat16)
    return jnp.dot(stacked, permutation, preferred_element_type=jnp.float32).astype(jnp.bfloat16)


def alive(place, count, live):
    lower = live // 2
    return (place < lower) | (place >= count - (live - lower))


def kernel(
    n_box,
    n_freq,
    live_ref,
    fine_ref,
    coarse_ref,
    table_ref,
    lists_fine_ref,
    lists_coarse_ref,
    out_fine_ref,
    out_coarse_ref,
    outbox,
    outbox_coarse,
    held,
    held_coarse,
    picks,
    weights,
    gathered,
    sums,
    send_sem,
    recv_sem,
    rim_send,
    rim_recv,
    coarse_send,
    coarse_recv,
    coarse_rim_send,
    coarse_rim_recv,
    far_send,
    far_recv,
    ready_sem,
    far_ready,
):
    box = lax.axis_index("box")
    col = lax.axis_index("freq")
    above = lax.rem(box + 1, n_box)
    below = lax.rem(box + n_box - 1, n_box)
    slots = table_ref.shape[0]
    groups = lists_fine_ref.shape[1]
    coarse_groups = lists_coarse_ref.shape[1]
    own = fine_ref.shape[0]
    rows = groups + 16
    live_fine = live_ref[0, 0]
    live_coarse = live_ref[0, 1]
    steps = tuple(range(1, n_freq))

    has_above, has_below = box < n_box - 1, box > 0
    far_above = has_above & (lax.rem(box, HALF) == HALF - 1)
    far_below = has_below & (lax.rem(box, HALF) == 0)
    near_above = has_above & (lax.rem(box, HALF) != HALF - 1)
    near_below = has_below & (lax.rem(box, HALF) != 0)
    gives_above = far_above & (col >= n_freq - 2)
    gives_below = far_below & (col < 2)

    early = lax.rem(box // HALF, 2) == 0

    def signal(semaphore, **device):
        pl.semaphore_signal(semaphore, inc=1, device_id=device)

    barrier = pltpu.get_barrier_semaphore()
    for near, other in ((near_above, above), (near_below, below)):

        @pl.when(near)
        def _():
            signal(barrier, box=other)

    for step in steps:

        @pl.when(jnp.logical_not(early) | (col + step < n_freq))
        def _():
            signal(barrier, freq=lax.rem(col + step, n_freq))

    for far, gives, other, giver in (
        (far_above, gives_above, above, 0),
        (far_below, gives_below, below, n_freq - 2),
    ):

        @pl.when(early & far)
        def _():
            for i in range(2):
                signal(barrier, box=other, freq=giver + i)

        @pl.when(early & gives)
        def _():
            for j in range(n_freq):
                signal(barrier, box=other, freq=j)

    late_ready = (
        n_freq
        - 1
        + jnp.where(far_above, 2, 0)
        + jnp.where(far_below, 2, 0)
        + jnp.where(gives_above, n_freq, 0)
        + jnp.where(gives_below, n_freq, 0)
    )
    ready = (
        jnp.where(early, col, late_ready)
        + near_above.astype(jnp.int32)
        + near_below.astype(jnp.int32)
    )

    permutation = interleave()

    place = col * own + lax.broadcasted_iota(jnp.int32, (own, 8, LANES), 0)
    fine_alive = alive(place, groups, live_fine)
    coarse_alive = alive(jnp.full((16, LANES), col, jnp.int32), coarse_groups, live_coarse)

    def cut(j, carry):
        lanes = pl.ds(pl.multiple_of(j * LANES, LANES), LANES)
        parts = [
            jnp.where(fine_alive, fine_ref[:, c, :, lanes].astype(jnp.float32), 0.0) for c in range(2)
        ]
        outbox[j] = by_band(parts, permutation).reshape(PAIRS, 2 * own, WIDE)
        both = jnp.concatenate(
            [coarse_ref[0, c, :, lanes].astype(jnp.float32) for c in range(2)], axis=0
        )
        outbox_coarse[j] = jnp.where(coarse_alive, both, 0.0).astype(jnp.bfloat16)
        return carry

    lax.fori_loop(0, n_freq, cut, 0, unroll=True)

    pl.semaphore_wait(barrier, ready)

    for step in steps:

        @pl.when(early & (col >= step))
        def _():
            signal(ready_sem.at[step], freq=col - step)

    for far, other, giver in ((far_above, above, 0), (far_below, below, n_freq - 2)):

        @pl.when(jnp.logical_not(early) & far)
        def _():
            for i in range(2):
                signal(far_ready, box=other, freq=giver + i)

    def coarse_copy(step):
        peer = lax.rem(col + step, n_freq)
        return pltpu.make_async_remote_copy(
            src_ref=outbox_coarse.at[peer],
            dst_ref=held_coarse.at[RIM_COARSE + col],
            send_sem=coarse_send.at[step],
            recv_sem=coarse_recv.at[step],
            device_id={"freq": peer},
        )

    def fine_copy(pair, step):
        peer = lax.rem(col + step, n_freq)
        return pltpu.make_async_remote_copy(
            src_ref=outbox.at[peer, pair],
            dst_ref=held.at[pair, 2 + col],
            send_sem=send_sem.at[pair, step],
            recv_sem=recv_sem.at[pair, step],
            device_id={"freq": peer},
        )

    def coarse_rim_copy(up):
        first, landing = (coarse_groups, 0) if up else (RIM_COARSE, RIM_COARSE + coarse_groups)
        return pltpu.make_async_remote_copy(
            src_ref=held_coarse.at[pl.ds(first, RIM_COARSE)],
            dst_ref=held_coarse.at[pl.ds(landing, RIM_COARSE)],
            send_sem=coarse_rim_send.at[int(up)],
            recv_sem=coarse_rim_recv.at[int(up)],
            device_id={"box": above if up else below},
        )

    def rim_copy(pair, up):
        first, landing = (n_freq, 0) if up else (2, 2 + n_freq)
        return pltpu.make_async_remote_copy(
            src_ref=held.at[pair, pl.ds(first, 2)],
            dst_ref=held.at[pair, pl.ds(landing, 2)],
            send_sem=rim_send.at[pair, int(up)],
            recv_sem=rim_recv.at[pair, int(up)],
            device_id={"box": above if up else below},
        )

    def far_copies(up, pair):
        if up:
            other, landing, index = above, col - (n_freq - 2), lax.rem(col, 2)
        else:
            other, landing, index = below, n_freq + 2 + col, lax.rem(col, 2)
        copies = []
        for j in range(n_freq):
            if pair is None:
                source, target = outbox_coarse.at[j], held_coarse.at[landing]
            else:
                source, target = outbox.at[j, pair], held.at[pair, landing]
            lot = PAIRS if pair is None else pair
            copies.append(
                pltpu.make_async_remote_copy(
                    src_ref=source,
                    dst_ref=target,
                    send_sem=far_send.at[int(up), lot, j],
                    recv_sem=far_recv.at[int(up), lot, index],
                    device_id={"box": other, "freq": j},
                )
            )
        return copies

    def far_wait(up, pair):
        for i in range(2):
            landing = i if up else n_freq + 2 + i
            if pair is None:
                here = held_coarse.at[landing]
            else:
                here = held.at[pair, landing]
            lot = PAIRS if pair is None else pair
            pltpu.make_async_copy(here, here, far_recv.at[int(up), lot, i]).wait()

    for pair in (None, *range(PAIRS)):
        for step in steps:

            @pl.when(col + step >= n_freq)
            def _():
                (coarse_copy(step) if pair is None else fine_copy(pair, step)).start()

    def send_on():
        for step in steps:

            @pl.when(col + step < n_freq)
            def _():
                @pl.when(early)
                def _():
                    pl.semaphore_wait(ready_sem.at[step], 1)

                coarse_copy(step).start()
                for pair in range(PAIRS):
                    fine_copy(pair, step).start()

        @pl.when(early & (gives_above | gives_below))
        def _():
            pl.semaphore_wait(far_ready, n_freq)

        for up, gives in ((True, gives_above), (False, gives_below)):

            @pl.when(gives)
            def _():
                for pair in (None, *range(PAIRS)):
                    for copy in far_copies(up, pair):
                        copy.start()

    held_coarse[RIM_COARSE + col] = outbox_coarse[col]
    for pair in range(PAIRS):
        held[pair, 2 + col] = outbox[col, pair]
        held[pair, 14] = jnp.zeros((16, WIDE), jnp.bfloat16)
        held[pair, 15] = jnp.zeros((16, WIDE), jnp.bfloat16)

    @pl.when(jnp.logical_not(has_below))
    def _():
        for pair in range(PAIRS):
            for i in range(2):
                held[pair, i] = jnp.zeros((16, WIDE), jnp.bfloat16)
        for i in range(2):
            held_coarse[i] = jnp.zeros((16, LANES), jnp.bfloat16)

    @pl.when(jnp.logical_not(has_above))
    def _():
        for pair in range(PAIRS):
            for i in range(2):
                held[pair, n_freq + 2 + i] = jnp.zeros((16, WIDE), jnp.bfloat16)
        for i in range(2):
            held_coarse[n_freq + 2 + i] = jnp.zeros((16, LANES), jnp.bfloat16)

    for blank in range(2 * RIM_COARSE + coarse_groups, 16):
        held_coarse[blank] = jnp.zeros((16, LANES), jnp.bfloat16)

    def prepare():
        fine_list = jnp.transpose(lists_fine_ref[...])
        fine_at = fine_list - (box * groups - RIM_FINE)
        fine_row = jnp.where(fine_list >= 0, (fine_at // 8) * 16 + fine_at % 8, -1000)
        coarse_list = jnp.transpose(lists_coarse_ref[...])
        coarse_at = coarse_list - (box * coarse_groups - RIM_COARSE)
        coarse_row = jnp.where(coarse_list >= 0, 192 + coarse_at, -1000)
        lane_fine = lax.broadcasted_iota(jnp.int32, (groups, WIDE), 1)
        lane_coarse = lax.broadcasted_iota(jnp.int32, (coarse_groups, WIDE), 1)
        no_rows = jnp.zeros((16 - coarse_groups, WIDE), jnp.float32)
        for k in range(slots):
            for odd in range(2):
                picks[odd, pl.ds(k * rows, groups)] = jnp.where(
                    fine_row[:, k : k + 1] + 8 * odd == lane_fine, 1.0, 0.0
                ).astype(jnp.bfloat16)
                coarse_hit = jnp.where(coarse_row[:, k : k + 1] + 16 * odd == lane_coarse, 1.0, 0.0)
                picks[odd, pl.ds(k * rows + groups, 16)] = jnp.concatenate(
                    [coarse_hit, no_rows], axis=0
                ).astype(jnp.bfloat16)

        lane_band = lax.broadcasted_iota(jnp.int32, (16, WIDE), 1) % BAND

        def widen(k, carry):
            table = [
                swap_blocks([table_ref[k, c, o].astype(jnp.float32) for o in range(8)]) for c in range(2)
            ]
            for g in range(BANDS):
                real, imag = table[0][g], table[1][g]
                full = jnp.concatenate(
                    [
                        jnp.concatenate([real, imag], axis=1),
                        jnp.concatenate([-imag, real], axis=1),
                    ],
                    axis=0,
                ).astype(jnp.bfloat16)
                for f in range(BAND):
                    weights[g, k, pl.ds(f * 16, 16)] = jnp.where(lane_band == f, full, jnp.zeros_like(full))
            return carry

        lax.fori_loop(0, slots, widen, 0, unroll=2)

    def middle(turn, carry):
        local = (turn == 0) == early

        @pl.when(local)
        def _():
            prepare()

        @pl.when(jnp.logical_not(local))
        def _():
            send_on()

        return carry

    lax.fori_loop(0, 2, middle, 0)

    def rim_start(copy):
        for up, near in ((True, near_above), (False, near_below)):

            @pl.when(near)
            def _():
                copy(up).start()

    def rim_wait(copy, pair):
        for up, near, far in ((True, near_below, far_below), (False, near_above, far_above)):

            @pl.when(near)
            def _():
                copy(up).wait_recv()

            @pl.when(far)
            def _():
                far_wait(up, pair)

    def arrive(pair):
        for step in steps:
            fine_copy(pair, step).wait_recv()
        rim_start(lambda up: rim_copy(pair, up))

    for step in steps:
        coarse_copy(step).wait_recv()
    rim_start(coarse_rim_copy)
    arrive(0)
    rim_wait(coarse_rim_copy, None)
    coarse_parts = [held_coarse[:, pl.ds(8 * c, 8)].astype(jnp.float32) for c in range(2)]
    coarse_bands = by_band(coarse_parts, permutation)
    for g in range(BANDS):
        held[g // 2, 12 + g % 2] = coarse_bands[16 * g : 16 * g + 16]

    def advance(pair, carry):
        @pl.when(pair < PAIRS - 1)
        def _():
            arrive(pair + 1)

        rim_wait(lambda up: rim_copy(pair, up), pair)
        sources = held[pair].reshape(16 * 16, WIDE)
        for odd in range(2):
            gathered[...] = jnp.dot(
                picks[odd], sources, preferred_element_type=jnp.float32
            ).astype(jnp.bfloat16)
            total = jnp.zeros((rows, WIDE), jnp.float32)
            for k in range(slots):
                total = total + jnp.dot(
                    gathered[pl.ds(k * rows, rows)],
                    weights[2 * pair + odd, k],
                    preferred_element_type=jnp.float32,
                )
            sums[2 * pair + odd] = total
        return carry

    lax.fori_loop(0, PAIRS, advance, 0)

    def back(first, live, count, scale):
        keep = alive(first + lax.broadcasted_iota(jnp.int32, (8, 8, LANES), 0), count, live)
        result = []
        for c in range(2):
            planes = swap_blocks(
                [sums[g, pl.ds(first + scale[1], 8), pl.ds(c * LANES, LANES)] for g in range(BANDS)]
            )
            turned = jnp.swapaxes(jnp.stack(planes, axis=0), 0, 1)
            result.append(jnp.where(keep, scale[0] * turned, 0.0).astype(jnp.bfloat16))
        return result

    def finish(part, carry):
        first = pl.multiple_of(part * 8, 8)
        result = back(first, live_fine, groups, (1.0, 0))
        for c in range(2):
            out_fine_ref[pl.ds(first, 8), c] = result[c]
        return carry

    lax.fori_loop(0, groups // 8, finish, 0, unroll=True)
    result = back(0, live_coarse, coarse_groups, (0.5, groups))
    for c in range(2):
        out_coarse_ref[:, c] = result[c]

    for step in steps:
        coarse_copy(step).wait_send()
        for pair in range(PAIRS):
            fine_copy(pair, step).wait_send()
    for up, near, gives in ((True, near_above, gives_above), (False, near_below, gives_below)):

        @pl.when(near)
        def _():
            coarse_rim_copy(up).wait_send()
            for pair in range(PAIRS):
                rim_copy(pair, up).wait_send()

        @pl.when(gives)
        def _():
            for pair in (None, *range(PAIRS)):
                for copy in far_copies(up, pair):
                    copy.wait_send()


def per_device(n_box, n_freq, spectra_fine, spectra_coarse, kernel_table, lists_fine, lists_coarse, live_counts):
    groups, slots = lists_fine.shape
    coarse_groups = lists_coarse.shape[0]
    own = spectra_fine.shape[0]
    rows = groups + 16
    vmem = pl.BlockSpec(memory_space=pltpu.VMEM)
    dma = pltpu.SemaphoreType.DMA
    return pl.pallas_call(
        functools.partial(kernel, n_box, n_freq),
        out_shape=(
            jax.ShapeDtypeStruct((groups, 2, 8, LANES), jnp.bfloat16),
            jax.ShapeDtypeStruct((coarse_groups, 2, 8, LANES), jnp.bfloat16),
        ),
        in_specs=[pl.BlockSpec(memory_space=pltpu.SMEM)] + [vmem] * 5,
        out_specs=(vmem, vmem),
        scratch_shapes=[
            pltpu.VMEM((n_freq, PAIRS, 2 * own, WIDE), jnp.bfloat16),
            pltpu.VMEM((n_freq, 16, LANES), jnp.bfloat16),
            pltpu.VMEM((PAIRS, 16, 16, WIDE), jnp.bfloat16),
            pltpu.VMEM((16, 16, LANES), jnp.bfloat16),
            pltpu.VMEM((2, slots * rows, WIDE), jnp.bfloat16),
            pltpu.VMEM((BANDS, slots, WIDE, WIDE), jnp.bfloat16),
            pltpu.VMEM((slots * rows, WIDE), jnp.bfloat16),
            pltpu.VMEM((BANDS, rows, WIDE), jnp.float32),
            dma((PAIRS, n_freq)),
            dma((PAIRS, n_freq)),
            dma((PAIRS, 2)),
            dma((PAIRS, 2)),
            dma((n_freq,)),
            dma((n_freq,)),
            dma((2,)),
            dma((2,)),
            dma((2, PAIRS + 1, n_freq)),
            dma((2, PAIRS + 1, 2)),
            pltpu.SemaphoreType.REGULAR((n_freq,)),
            pltpu.SemaphoreType.REGULAR,
        ],
        compiler_params=pltpu.CompilerParams(
            collective_id=0, has_side_effects=True, vmem_limit_bytes=56 * 1024 * 1024
        ),
    )(live_counts, spectra_fine, spectra_coarse, kernel_table, lists_fine.T, lists_coarse.T)


def solution(mesh):
    return jax.shard_map(
        functools.partial(per_device, mesh.shape["box"], mesh.shape["freq"]),
        mesh=mesh,
        in_specs=(
            P(("box", "freq"), None, None, None),
            P(("box", "freq"), None, None, None),
            P(None, None, None, None, "freq"),
            P("box", None),
            P("box", None),
            P("box", None),
        ),
        out_specs=(P("box", None, None, "freq"), P("box", None, None, "freq")),
        check_vma=False,
    )
```

```python
import functools

import jax
import jax.numpy as jnp
from jax import lax
from jax.experimental import pallas as pl
from jax.experimental.pallas import tpu as pltpu
from jax.sharding import PartitionSpec as P

RIM_FINE = 16
RIM_COARSE = 2
HALF = 8
LANES = 128
BAND = 16
BANDS = LANES // BAND
PAIRS = BANDS // 2
WIDE = 2 * 8 * BAND
HALF_BAND = BAND // 2
FIRST = LANES
PACK = FIRST + PAIRS * WIDE
PARTS = ((0, FIRST + 2 * WIDE), (FIRST + 2 * WIDE, 2 * WIDE))


def swap_blocks(planes):
    count = len(planes)
    width = LANES // count
    block = lax.broadcasted_iota(jnp.int32, planes[0].shape, 1) // width
    planes = list(planes)
    step = count // 2
    while step:
        upper = (block & step) != 0
        for p in range(count):
            if p & step == 0:
                first, second = planes[p], planes[p + step]
                planes[p] = jnp.where(upper, pltpu.roll(second, width * step, 1), first)
                planes[p + step] = jnp.where(upper, second, pltpu.roll(first, LANES - width * step, 1))
        step //= 2
    return planes


def interleave():
    row = lax.broadcasted_iota(jnp.int32, (WIDE, WIDE), 0)
    lane = lax.broadcasted_iota(jnp.int32, (WIDE, WIDE), 1)
    hit = (row // BAND == lane % BAND) & (row % BAND == lane // BAND)
    return jnp.where(hit, 1.0, 0.0).astype(jnp.bfloat16)


def by_band(parts, permutation):
    planes = []
    for part in parts:
        turned = jnp.swapaxes(part, 0, 1)
        planes.append(swap_blocks([turned[i] for i in range(8)]))
    stacked = jnp.concatenate(
        [jnp.concatenate([planes[0][g], planes[1][g]], axis=1) for g in range(BANDS)], axis=0
    ).astype(jnp.bfloat16)
    return jnp.dot(stacked, permutation, preferred_element_type=jnp.float32).astype(jnp.bfloat16)


def alive(place, count, live):
    lower = live // 2
    return (place < lower) | (place >= count - (live - lower))


def kernel(
    n_box,
    n_freq,
    live_ref,
    fine_ref,
    coarse_ref,
    table_ref,
    lists_fine_ref,
    lists_coarse_ref,
    sums,
    outbox,
    held,
    picks,
    weights,
    gathered0,
    gathered1,
    send_sem,
    recv_sem,
    rim_send,
    rim_recv,
    far_send,
    far_recv,
    ready_sem,
    far_ready,
):
    box = lax.axis_index("box")
    col = lax.axis_index("freq")
    above = lax.rem(box + 1, n_box)
    below = lax.rem(box + n_box - 1, n_box)
    slots = table_ref.shape[0]
    groups = lists_fine_ref.shape[1]
    coarse_groups = lists_coarse_ref.shape[0]
    own = fine_ref.shape[0]
    rows = groups + 16
    live_fine = live_ref[0, 0]
    live_coarse = live_ref[0, 1]
    steps = tuple(range(1, n_freq))
    order = (4, 3, 5, 2, 6, 1, 7)

    has_above, has_below = box < n_box - 1, box > 0
    far_above = has_above & (lax.rem(box, HALF) == HALF - 1)
    far_below = has_below & (lax.rem(box, HALF) == 0)
    near_above = has_above & (lax.rem(box, HALF) != HALF - 1)
    near_below = has_below & (lax.rem(box, HALF) != 0)
    gives_above = far_above & (col >= n_freq - 2)
    gives_below = far_below & (col < 2)

    early = lax.rem(box // HALF, 2) == 0
    late = jnp.logical_not(early)

    def signal(semaphore, **device):
        pl.semaphore_signal(semaphore, inc=1, device_id=device)

    barrier = pltpu.get_barrier_semaphore()
    for near, other in ((near_above, above), (near_below, below)):

        @pl.when(near)
        def _():
            signal(barrier, box=other)

    for step in steps:

        @pl.when(late | (col + step < n_freq))
        def _():
            signal(barrier, freq=lax.rem(col + step, n_freq))

    for far, gives, other, giver in (
        (far_above, gives_above, above, 0),
        (far_below, gives_below, below, n_freq - 2),
    ):

        @pl.when(early & far)
        def _():
            for i in range(2):
                signal(barrier, box=other, freq=giver + i)

        @pl.when(early & gives)
        def _():
            for j in range(n_freq):
                signal(barrier, box=other, freq=j)

    late_ready = (
        n_freq
        - 1
        + jnp.where(far_above, 2, 0)
        + jnp.where(far_below, 2, 0)
        + jnp.where(gives_above, n_freq, 0)
        + jnp.where(gives_below, n_freq, 0)
    )
    ready = (
        jnp.where(early, col, late_ready)
        + near_above.astype(jnp.int32)
        + near_below.astype(jnp.int32)
    )

    permutation = interleave()

    place = col * own + lax.broadcasted_iota(jnp.int32, (own, 8, LANES), 0)
    fine_alive = alive(place, groups, live_fine)
    coarse_alive = alive(jnp.full((16, LANES), col, jnp.int32), coarse_groups, live_coarse)

    def cut(j, carry):
        lanes = pl.ds(pl.multiple_of(j * LANES, LANES), LANES)
        parts = [
            jnp.where(fine_alive, fine_ref[:, c, :, lanes].astype(jnp.float32), 0.0) for c in range(2)
        ]
        bands = by_band(parts, permutation)
        both = jnp.concatenate(
            [coarse_ref[0, c, :, lanes].astype(jnp.float32) for c in range(2)], axis=0
        )
        both = jnp.where(coarse_alive, both, 0.0).astype(jnp.bfloat16)
        rows_of = [bands[16 * pair : 16 * pair + 16] for pair in range(PAIRS)]
        outbox[j] = jnp.concatenate([both, *rows_of], axis=1)
        return carry

    lax.fori_loop(0, n_freq, cut, 0, unroll=True)

    pl.semaphore_wait(barrier, ready)

    for step in steps:

        @pl.when(early & (col >= step))
        def _():
            signal(ready_sem.at[step], freq=col - step)

    for far, other, giver in ((far_above, above, 0), (far_below, below, n_freq - 2)):

        @pl.when(late & far)
        def _():
            for i in range(2):
                signal(far_ready, box=other, freq=giver + i)

    def lanes_of(part):
        return pl.ds(PARTS[part][0], PARTS[part][1])

    def swap_copy(part, step):
        peer = lax.rem(col + step, n_freq)
        return pltpu.make_async_remote_copy(
            src_ref=outbox.at[peer, :, lanes_of(part)],
            dst_ref=held.at[2 + col, :, lanes_of(part)],
            send_sem=send_sem.at[part, step],
            recv_sem=recv_sem.at[part, step],
            device_id={"freq": peer},
        )

    def rim_copy(part, up):
        first, landing = (n_freq, 0) if up else (2, 2 + n_freq)
        return pltpu.make_async_remote_copy(
            src_ref=held.at[pl.ds(first, 2), :, lanes_of(part)],
            dst_ref=held.at[pl.ds(landing, 2), :, lanes_of(part)],
            send_sem=rim_send.at[part, int(up)],
            recv_sem=rim_recv.at[part, int(up)],
            device_id={"box": above if up else below},
        )

    def far_copies(up, part):
        if up:
            other, landing = above, col - (n_freq - 2)
        else:
            other, landing = below, n_freq + 2 + col
        return [
            pltpu.make_async_remote_copy(
                src_ref=outbox.at[j, :, lanes_of(part)],
                dst_ref=held.at[landing, :, lanes_of(part)],
                send_sem=far_send.at[int(up), part, j],
                recv_sem=far_recv.at[int(up), part, lax.rem(col, 2)],
                device_id={"box": other, "freq": j},
            )
            for j in range(n_freq)
        ]

    def far_wait(up, part):
        for i in range(2):
            here = held.at[i if up else n_freq + 2 + i, :, lanes_of(part)]
            pltpu.make_async_copy(here, here, far_recv.at[int(up), part, i]).wait()

    def far_start(when):
        for up, gives in ((True, gives_above), (False, gives_below)):

            @pl.when(when & gives)
            def _():
                for part in range(len(PARTS)):
                    for copy in far_copies(up, part):
                        copy.start()

    far_start(late)
    for part in range(len(PARTS)):
        for step in order:

            @pl.when(late | (col + step >= n_freq))
            def _():
                swap_copy(part, step).start()

    def send_on():
        for step in steps:

            @pl.when(early & (col + step < n_freq))
            def _():
                pl.semaphore_wait(ready_sem.at[step], 1)
                for part in range(len(PARTS)):
                    swap_copy(part, step).start()

        @pl.when(early & (gives_above | gives_below))
        def _():
            pl.semaphore_wait(far_ready, n_freq)

        far_start(early)

    held[2 + col] = outbox[col]
    blank = jnp.zeros((16, PACK), jnp.bfloat16)
    for i in range(n_freq + 4, 16):
        held[i] = blank

    @pl.when(jnp.logical_not(has_below))
    def _():
        for i in range(2):
            held[i] = blank

    @pl.when(jnp.logical_not(has_above))
    def _():
        for i in range(2):
            held[n_freq + 2 + i] = blank

    def prepare():
        fine_list = jnp.transpose(lists_fine_ref[...])
        fine_at = fine_list - (box * groups - RIM_FINE)
        fine_row = jnp.where(fine_list >= 0, (fine_at // 8) * 16 + fine_at % 8, -1000)
        coarse_list = lists_coarse_ref[...]
        coarse_at = coarse_list - (box * coarse_groups - RIM_COARSE)
        coarse_row = jnp.where(coarse_list >= 0, 192 + coarse_at, -1000)
        lane_fine = lax.broadcasted_iota(jnp.int32, (groups, WIDE), 1)
        lane_coarse = lax.broadcasted_iota(jnp.int32, (coarse_groups, WIDE), 1)
        no_rows = jnp.zeros((16 - coarse_groups, WIDE), jnp.float32)
        for k in range(slots):
            for odd in range(2):
                picks[odd, pl.ds(k * rows, groups)] = jnp.where(
                    fine_row[:, k : k + 1] + 8 * odd == lane_fine, 1.0, 0.0
                ).astype(jnp.bfloat16)
                coarse_hit = jnp.where(coarse_row[:, k : k + 1] + 16 * odd == lane_coarse, 1.0, 0.0)
                picks[odd, pl.ds(k * rows + groups, 16)] = jnp.concatenate(
                    [coarse_hit, no_rows], axis=0
                ).astype(jnp.bfloat16)

        lane = lax.broadcasted_iota(jnp.int32, (16, LANES), 1) % HALF_BAND
        left = lax.broadcasted_iota(jnp.int32, (8, LANES), 1) < LANES // 2

        def widen(pair, carry):
            for i in range(2):
                planes = [
                    table_ref[2 * pair + i, c, o].astype(jnp.float32)
                    for c in range(2)
                    for o in range(8)
                ]
                for b, real in enumerate(swap_blocks(planes)):
                    turned = pltpu.roll(real, LANES // 2, 1)
                    imag = jnp.where(left, -turned, turned)
                    full = jnp.concatenate([real, imag], axis=0).astype(jnp.bfloat16)
                    for f in range(HALF_BAND):
                        weights[b, pair, pl.ds(i * LANES + f * 16, 16)] = jnp.where(
                            lane == f, full, jnp.zeros_like(full)
                        )
            return carry

        lax.fori_loop(0, slots // 2, widen, 0)

    def middle(turn, carry):
        local = (turn == 0) == (early & (col < n_freq // 2))

        @pl.when(local)
        def _():
            prepare()

        @pl.when(jnp.logical_not(local))
        def _():
            send_on()

        return carry

    lax.fori_loop(0, 2, middle, 0)

    def rim_wait(part):
        for up, near, far in ((True, near_below, far_below), (False, near_above, far_above)):

            @pl.when(near)
            def _():
                rim_copy(part, up).wait_recv()

            @pl.when(far)
            def _():
                far_wait(up, part)

    def arrive(part):
        for senders, up, near in (
            ((0, 1), False, near_below),
            ((n_freq - 2, n_freq - 1), True, near_above),
            (range(2, n_freq - 2), None, None),
        ):
            for j in senders:
                step = lax.rem(col + n_freq - j, n_freq)

                @pl.when(step > 0)
                def _():
                    swap_copy(part, step).wait_recv()

            if near is not None:

                @pl.when(near)
                def _():
                    rim_copy(part, up).start()

    arrive(0)
    rim_wait(0)
    raw = held[:, :, pl.ds(0, LANES)].astype(jnp.float32)
    coarse_bands = by_band([raw[:, 0:8], raw[:, 8:16]], permutation)
    for g in range(BANDS):
        held[n_freq + 4 + g % 2, :, pl.ds(FIRST + g // 2 * WIDE, WIDE)] = coarse_bands[16 * g : 16 * g + 16]

    def advance(pair, carry):
        @pl.when(pair == 1)
        def _():
            arrive(1)

        @pl.when(pair == 2)
        def _():
            rim_wait(1)

        lanes = pl.ds(pl.multiple_of(FIRST + pair * WIDE, LANES), WIDE)
        sources = held[:, :, lanes].reshape(16 * 16, WIDE)
        for odd, gathered in enumerate((gathered0, gathered1)):
            for m in range(0, slots * rows, 416):
                gathered[pl.ds(m, 416)] = jnp.dot(
                    picks[odd, pl.ds(m, 416)], sources, preferred_element_type=jnp.float32
                ).astype(jnp.bfloat16)
        for odd, gathered in enumerate((gathered0, gathered1)):
            for half in range(2):
                band = 4 * pair + 2 * odd + half
                side = pl.ds(half * LANES, LANES)
                total = jnp.zeros((rows, LANES), jnp.float32)
                for k in range(0, slots, 2):
                    both = jnp.concatenate(
                        [gathered[pl.ds((k + i) * rows, rows), side] for i in range(2)], axis=1
                    )
                    total = total + jnp.dot(
                        both, weights[band, k // 2], preferred_element_type=jnp.float32
                    )
                sums[band] = total
        return carry

    lax.fori_loop(0, PAIRS, advance, 0)

    for part in range(len(PARTS)):
        for step in steps:
            swap_copy(part, step).wait_send()
        for up, near, gives in ((True, near_above, gives_above), (False, near_below, gives_below)):

            @pl.when(near)
            def _():
                rim_copy(part, up).wait_send()

            @pl.when(gives)
            def _():
                for copy in far_copies(up, part):
                    copy.wait_send()


def unfold(live_ref, sums_ref, out_fine_ref, out_coarse_ref):
    groups = out_fine_ref.shape[0]
    coarse_groups = out_coarse_ref.shape[0]

    def back(first, place, live, count, scale):
        keep = alive(place + lax.broadcasted_iota(jnp.int32, (8, 8, LANES), 0), count, live)
        planes = swap_blocks([sums_ref[b, pl.ds(first, 8)] for b in range(2 * BANDS)])
        result = []
        for c in range(2):
            turned = jnp.swapaxes(jnp.stack(planes[8 * c : 8 * c + 8], axis=0), 0, 1)
            result.append(jnp.where(keep, scale * turned, 0.0).astype(jnp.bfloat16))
        return result

    for first in range(0, groups, 8):
        result = back(first, first, live_ref[0, 0], groups, 1.0)
        for c in range(2):
            out_fine_ref[pl.ds(first, 8), c] = result[c]
    result = back(groups, 0, live_ref[0, 1], coarse_groups, 0.5)
    for c in range(2):
        out_coarse_ref[:, c] = result[c]


def per_device(n_box, n_freq, spectra_fine, spectra_coarse, kernel_table, lists_fine, lists_coarse, live_counts):
    groups, slots = lists_fine.shape
    coarse_groups = lists_coarse.shape[0]
    own = spectra_fine.shape[0]
    rows = groups + 16
    vmem = pl.BlockSpec(memory_space=pltpu.VMEM)
    dma = pltpu.SemaphoreType.DMA
    sums = pl.pallas_call(
        functools.partial(kernel, n_box, n_freq),
        out_shape=jax.ShapeDtypeStruct((2 * BANDS, rows, LANES), jnp.float32),
        in_specs=[pl.BlockSpec(memory_space=pltpu.SMEM)] + [vmem] * 5,
        out_specs=vmem,
        scratch_shapes=[
            pltpu.VMEM((n_freq, 2 * own, PACK), jnp.bfloat16),
            pltpu.VMEM((16, 16, PACK), jnp.bfloat16),
            pltpu.VMEM((2, slots * rows, WIDE), jnp.bfloat16),
            pltpu.VMEM((2 * BANDS, slots // 2, WIDE, LANES), jnp.bfloat16),
            pltpu.VMEM((slots * rows, WIDE), jnp.bfloat16),
            pltpu.VMEM((slots * rows, WIDE), jnp.bfloat16),
            dma((len(PARTS), n_freq)),
            dma((len(PARTS), n_freq)),
            dma((len(PARTS), 2)),
            dma((len(PARTS), 2)),
            dma((2, len(PARTS), n_freq)),
            dma((2, len(PARTS), 2)),
            pltpu.SemaphoreType.REGULAR((n_freq,)),
            pltpu.SemaphoreType.REGULAR,
        ],
        compiler_params=pltpu.CompilerParams(
            collective_id=0, has_side_effects=True, vmem_limit_bytes=56 * 1024 * 1024
        ),
    )(live_counts, spectra_fine, spectra_coarse, kernel_table, lists_fine.T, lists_coarse)
    return pl.pallas_call(
        unfold,
        out_shape=(
            jax.ShapeDtypeStruct((groups, 2, 8, LANES), jnp.bfloat16),
            jax.ShapeDtypeStruct((coarse_groups, 2, 8, LANES), jnp.bfloat16),
        ),
        in_specs=[pl.BlockSpec(memory_space=pltpu.SMEM), vmem],
        out_specs=(vmem, vmem),
        compiler_params=pltpu.CompilerParams(vmem_limit_bytes=16 * 1024 * 1024),
    )(live_counts, sums)


def solution(mesh):
    return jax.shard_map(
        functools.partial(per_device, mesh.shape["box"], mesh.shape["freq"]),
        mesh=mesh,
        in_specs=(
            P(("box", "freq"), None, None, None),
            P(("box", "freq"), None, None, None),
            P(None, None, None, None, "freq"),
            P("box", None),
            P("box", None),
            P("box", None),
        ),
        out_specs=(P("box", None, None, "freq"), P("box", None, None, "freq")),
        check_vma=False,
    )
```

```python
import functools

import jax
import jax.numpy as jnp
from jax import lax
from jax.experimental import pallas as pl
from jax.experimental.pallas import tpu as pltpu
from jax.sharding import PartitionSpec as P

RIM_FINE = 16
RIM_COARSE = 2
HALF = 8
LANES = 128
BAND = 16
BANDS = LANES // BAND
PAIRS = BANDS // 2
WIDE = 2 * 8 * BAND
HALF_BAND = BAND // 2
FIRST = LANES
PACK = FIRST + PAIRS * WIDE
PARTS = ((0, FIRST + 2 * WIDE), (FIRST + 2 * WIDE, 2 * WIDE))


def swap_blocks(planes):
    count = len(planes)
    width = LANES // count
    block = lax.broadcasted_iota(jnp.int32, planes[0].shape, 1) // width
    planes = list(planes)
    step = count // 2
    while step:
        upper = (block & step) != 0
        for p in range(count):
            if p & step == 0:
                first, second = planes[p], planes[p + step]
                planes[p] = jnp.where(upper, pltpu.roll(second, width * step, 1), first)
                planes[p + step] = jnp.where(upper, second, pltpu.roll(first, LANES - width * step, 1))
        step //= 2
    return planes


def interleave():
    row = lax.broadcasted_iota(jnp.int32, (WIDE, WIDE), 0)
    lane = lax.broadcasted_iota(jnp.int32, (WIDE, WIDE), 1)
    hit = (row // BAND == lane % BAND) & (row % BAND == lane // BAND)
    return jnp.where(hit, 1.0, 0.0).astype(jnp.bfloat16)


def by_band(parts, permutation):
    planes = []
    for part in parts:
        turned = jnp.swapaxes(part, 0, 1)
        planes.append(swap_blocks([turned[i] for i in range(8)]))
    stacked = jnp.concatenate(
        [jnp.concatenate([planes[0][g], planes[1][g]], axis=1) for g in range(BANDS)], axis=0
    ).astype(jnp.bfloat16)
    return jnp.dot(stacked, permutation, preferred_element_type=jnp.float32).astype(jnp.bfloat16)


def alive(place, count, live):
    lower = live // 2
    return (place < lower) | (place >= count - (live - lower))


def kernel(
    n_box,
    n_freq,
    live_ref,
    fine_hbm,
    coarse_hbm,
    table_hbm,
    lists_fine_hbm,
    lists_coarse_hbm,
    out_fine_hbm,
    out_coarse_hbm,
    out_fine_ref,
    out_coarse_ref,
    sums,
    store_sem,
    fine_ref,
    coarse_ref,
    table_ref,
    lists_fine_ref,
    lists_coarse_ref,
    load_sem,
    outbox,
    held,
    picks,
    weights,
    gathered0,
    gathered1,
    send_sem,
    recv_sem,
    rim_send,
    rim_recv,
    far_send,
    far_recv,
    ready_sem,
    far_ready,
):
    box = lax.axis_index("box")
    col = lax.axis_index("freq")
    above = lax.rem(box + 1, n_box)
    below = lax.rem(box + n_box - 1, n_box)
    slots = table_ref.shape[0]
    groups = lists_fine_ref.shape[1]
    coarse_groups = lists_coarse_ref.shape[0]
    own = fine_ref.shape[0]
    rows = groups + 16
    live_fine = live_ref[0, 0]
    live_coarse = live_ref[0, 1]
    steps = tuple(range(1, n_freq))
    order = (4, 3, 5, 2, 6, 1, 7)

    has_above, has_below = box < n_box - 1, box > 0
    far_above = has_above & (lax.rem(box, HALF) == HALF - 1)
    far_below = has_below & (lax.rem(box, HALF) == 0)
    near_above = has_above & (lax.rem(box, HALF) != HALF - 1)
    near_below = has_below & (lax.rem(box, HALF) != 0)
    gives_above = far_above & (col >= n_freq - 2)
    gives_below = far_below & (col < 2)

    early = lax.rem(box // HALF, 2) == 0
    late = jnp.logical_not(early)

    def signal(semaphore, **device):
        pl.semaphore_signal(semaphore, inc=1, device_id=device)

    loads = [
        pltpu.make_async_copy(source, target, load_sem.at[i])
        for i, (source, target) in enumerate(
            (
                (fine_hbm, fine_ref),
                (coarse_hbm, coarse_ref),
                (lists_fine_hbm, lists_fine_ref),
                (lists_coarse_hbm, lists_coarse_ref),
                (table_hbm, table_ref),
            )
        )
    ]
    for load in loads:
        load.start()

    barrier = pltpu.get_barrier_semaphore()
    for near, other in ((near_above, above), (near_below, below)):

        @pl.when(near)
        def _():
            signal(barrier, box=other)

    for step in steps:

        @pl.when(late | (col + step < n_freq))
        def _():
            signal(barrier, freq=lax.rem(col + step, n_freq))

    for far, gives, other, giver in (
        (far_above, gives_above, above, 0),
        (far_below, gives_below, below, n_freq - 2),
    ):

        @pl.when(early & far)
        def _():
            for i in range(2):
                signal(barrier, box=other, freq=giver + i)

        @pl.when(early & gives)
        def _():
            for j in range(n_freq):
                signal(barrier, box=other, freq=j)

    late_ready = (
        n_freq
        - 1
        + jnp.where(far_above, 2, 0)
        + jnp.where(far_below, 2, 0)
        + jnp.where(gives_above, n_freq, 0)
        + jnp.where(gives_below, n_freq, 0)
    )
    ready = (
        jnp.where(early, col, late_ready)
        + near_above.astype(jnp.int32)
        + near_below.astype(jnp.int32)
    )

    permutation = interleave()

    place = col * own + lax.broadcasted_iota(jnp.int32, (own, 8, LANES), 0)
    fine_alive = alive(place, groups, live_fine)
    coarse_alive = alive(jnp.full((16, LANES), col, jnp.int32), coarse_groups, live_coarse)

    def cut(j, carry):
        lanes = pl.ds(pl.multiple_of(j * LANES, LANES), LANES)
        parts = [
            jnp.where(fine_alive, fine_ref[:, c, :, lanes].astype(jnp.float32), 0.0) for c in range(2)
        ]
        bands = by_band(parts, permutation)
        both = jnp.concatenate(
            [coarse_ref[0, c, :, lanes].astype(jnp.float32) for c in range(2)], axis=0
        )
        both = jnp.where(coarse_alive, both, 0.0).astype(jnp.bfloat16)
        rows_of = [bands[16 * pair : 16 * pair + 16] for pair in range(PAIRS)]
        outbox[j] = jnp.concatenate([both, *rows_of], axis=1)
        return carry

    for load in loads[:2]:
        load.wait()
    lax.fori_loop(0, n_freq, cut, 0, unroll=True)

    pl.semaphore_wait(barrier, ready)

    for step in steps:

        @pl.when(early & (col >= step))
        def _():
            signal(ready_sem.at[step], freq=col - step)

    for far, other, giver in ((far_above, above, 0), (far_below, below, n_freq - 2)):

        @pl.when(late & far)
        def _():
            for i in range(2):
                signal(far_ready, box=other, freq=giver + i)

    def lanes_of(part):
        return pl.ds(PARTS[part][0], PARTS[part][1])

    def swap_copy(part, step):
        peer = lax.rem(col + step, n_freq)
        return pltpu.make_async_remote_copy(
            src_ref=outbox.at[peer, :, lanes_of(part)],
            dst_ref=held.at[2 + col, :, lanes_of(part)],
            send_sem=send_sem.at[part, step],
            recv_sem=recv_sem.at[part, step],
            device_id={"freq": peer},
        )

    def rim_copy(part, up):
        first, landing = (n_freq, 0) if up else (2, 2 + n_freq)
        return pltpu.make_async_remote_copy(
            src_ref=held.at[pl.ds(first, 2), :, lanes_of(part)],
            dst_ref=held.at[pl.ds(landing, 2), :, lanes_of(part)],
            send_sem=rim_send.at[part, int(up)],
            recv_sem=rim_recv.at[part, int(up)],
            device_id={"box": above if up else below},
        )

    def far_copies(up, part):
        if up:
            other, landing = above, col - (n_freq - 2)
        else:
            other, landing = below, n_freq + 2 + col
        return [
            pltpu.make_async_remote_copy(
                src_ref=outbox.at[j, :, lanes_of(part)],
                dst_ref=held.at[landing, :, lanes_of(part)],
                send_sem=far_send.at[int(up), part, j],
                recv_sem=far_recv.at[int(up), part, lax.rem(col, 2)],
                device_id={"box": other, "freq": j},
            )
            for j in range(n_freq)
        ]

    def far_wait(up, part):
        for i in range(2):
            here = held.at[i if up else n_freq + 2 + i, :, lanes_of(part)]
            pltpu.make_async_copy(here, here, far_recv.at[int(up), part, i]).wait()

    def far_start(when):
        for up, gives in ((True, gives_above), (False, gives_below)):

            @pl.when(when & gives)
            def _():
                for part in range(len(PARTS)):
                    for copy in far_copies(up, part):
                        copy.start()

    far_start(late)
    for part in range(len(PARTS)):
        for step in order:

            @pl.when(late | (col + step >= n_freq))
            def _():
                swap_copy(part, step).start()

    def send_on():
        for step in steps:

            @pl.when(early & (col + step < n_freq))
            def _():
                pl.semaphore_wait(ready_sem.at[step], 1)
                for part in range(len(PARTS)):
                    swap_copy(part, step).start()

        @pl.when(early & (gives_above | gives_below))
        def _():
            pl.semaphore_wait(far_ready, n_freq)

        far_start(early)

    held[2 + col] = outbox[col]
    blank = jnp.zeros((16, PACK), jnp.bfloat16)
    for i in range(n_freq + 4, 16):
        held[i] = blank

    @pl.when(jnp.logical_not(has_below))
    def _():
        for i in range(2):
            held[i] = blank

    @pl.when(jnp.logical_not(has_above))
    def _():
        for i in range(2):
            held[n_freq + 2 + i] = blank

    def prepare():
        for load in loads[2:]:
            load.wait()
        fine_list = jnp.transpose(lists_fine_ref[...])
        fine_at = fine_list - (box * groups - RIM_FINE)
        fine_row = jnp.where(fine_list >= 0, (fine_at // 8) * 16 + fine_at % 8, -1000)
        coarse_list = lists_coarse_ref[...]
        coarse_at = coarse_list - (box * coarse_groups - RIM_COARSE)
        coarse_row = jnp.where(coarse_list >= 0, 192 + coarse_at, -1000)
        lane_fine = lax.broadcasted_iota(jnp.int32, (groups, WIDE), 1)
        lane_coarse = lax.broadcasted_iota(jnp.int32, (coarse_groups, WIDE), 1)
        no_rows = jnp.zeros((16 - coarse_groups, WIDE), jnp.float32)
        for k in range(slots):
            for odd in range(2):
                picks[odd, pl.ds(k * rows, groups)] = jnp.where(
                    fine_row[:, k : k + 1] + 8 * odd == lane_fine, 1.0, 0.0
                ).astype(jnp.bfloat16)
                coarse_hit = jnp.where(coarse_row[:, k : k + 1] + 16 * odd == lane_coarse, 1.0, 0.0)
                picks[odd, pl.ds(k * rows + groups, 16)] = jnp.concatenate(
                    [coarse_hit, no_rows], axis=0
                ).astype(jnp.bfloat16)

        lane = lax.broadcasted_iota(jnp.int32, (16, LANES), 1) % HALF_BAND
        left = lax.broadcasted_iota(jnp.int32, (8, LANES), 1) < LANES // 2

        def widen(pair, carry):
            for i in range(2):
                planes = [
                    table_ref[2 * pair + i, c, o].astype(jnp.float32)
                    for c in range(2)
                    for o in range(8)
                ]
                for b, real in enumerate(swap_blocks(planes)):
                    turned = pltpu.roll(real, LANES // 2, 1)
                    imag = jnp.where(left, -turned, turned)
                    full = jnp.concatenate([real, imag], axis=0).astype(jnp.bfloat16)
                    for f in range(HALF_BAND):
                        weights[b, pair, pl.ds(i * LANES + f * 16, 16)] = jnp.where(
                            lane == f, full, jnp.zeros_like(full)
                        )
            return carry

        lax.fori_loop(0, slots // 2, widen, 0)

    def middle(turn, carry):
        local = (turn == 0) == (early & (col < 2))

        @pl.when(local)
        def _():
            prepare()

        @pl.when(jnp.logical_not(local))
        def _():
            send_on()

        return carry

    lax.fori_loop(0, 2, middle, 0)

    def rim_wait(part):
        for up, near, far in ((True, near_below, far_below), (False, near_above, far_above)):

            @pl.when(near)
            def _():
                rim_copy(part, up).wait_recv()

            @pl.when(far)
            def _():
                far_wait(up, part)

    def arrive(part):
        for senders, up, near in (
            ((0, 1), False, near_below),
            ((n_freq - 2, n_freq - 1), True, near_above),
            (range(2, n_freq - 2), None, None),
        ):
            for j in senders:
                step = lax.rem(col + n_freq - j, n_freq)

                @pl.when(step > 0)
                def _():
                    swap_copy(part, step).wait_recv()

            if near is not None:

                @pl.when(near)
                def _():
                    rim_copy(part, up).start()

    arrive(0)
    rim_wait(0)
    raw = held[:, :, pl.ds(0, LANES)].astype(jnp.float32)
    coarse_bands = by_band([raw[:, 0:8], raw[:, 8:16]], permutation)
    for g in range(BANDS):
        held[n_freq + 4 + g % 2, :, pl.ds(FIRST + g // 2 * WIDE, WIDE)] = coarse_bands[16 * g : 16 * g + 16]

    def advance(pair, carry):
        @pl.when(pair == 1)
        def _():
            arrive(1)

        @pl.when(pair == 2)
        def _():
            rim_wait(1)

        lanes = pl.ds(pl.multiple_of(FIRST + pair * WIDE, LANES), WIDE)
        sources = held[:, :, lanes].reshape(16 * 16, WIDE)
        for odd, gathered in enumerate((gathered0, gathered1)):
            for m in range(0, slots * rows, 416):
                gathered[pl.ds(m, 416)] = jnp.dot(
                    picks[odd, pl.ds(m, 416)], sources, preferred_element_type=jnp.float32
                ).astype(jnp.bfloat16)
        for odd, gathered in enumerate((gathered0, gathered1)):
            for half in range(2):
                band = 4 * pair + 2 * odd + half
                side = pl.ds(half * LANES, LANES)
                total = jnp.zeros((rows, LANES), jnp.float32)
                for k in range(0, slots, 2):
                    both = jnp.concatenate(
                        [gathered[pl.ds((k + i) * rows, rows), side] for i in range(2)], axis=1
                    )
                    total = total + jnp.dot(
                        both, weights[band, k // 2], preferred_element_type=jnp.float32
                    )
                sums[band] = total
        return carry

    lax.fori_loop(0, PAIRS, advance, 0)

    def back(first, place, live, count, scale):
        keep = alive(place + lax.broadcasted_iota(jnp.int32, (16, 8, LANES), 0), count, live)
        planes = swap_blocks([sums[b, pl.ds(first, 16)] for b in range(2 * BANDS)])
        result = []
        for c in range(2):
            turned = jnp.swapaxes(jnp.stack(planes[8 * c : 8 * c + 8], axis=0), 0, 1)
            result.append(jnp.where(keep, scale * turned, 0.0).astype(jnp.bfloat16))
        return result

    stores = []
    result = back(groups, 0, live_coarse, coarse_groups, 0.5)
    for c in range(2):
        out_coarse_ref[:, c] = result[c][:coarse_groups]
    stores.append(pltpu.make_async_copy(out_coarse_ref, out_coarse_hbm, store_sem.at[0]))
    stores[-1].start()
    for first in range(0, groups, 16):
        result = back(first, first, live_fine, groups, 1.0)
        part = pl.ds(first, 16)
        for c in range(2):
            out_fine_ref[part, c] = result[c]
        stores.append(
            pltpu.make_async_copy(
                out_fine_ref.at[part], out_fine_hbm.at[part], store_sem.at[first // 16 + 1]
            )
        )
        stores[-1].start()
    for store in stores:
        store.wait()

    for part in range(len(PARTS)):
        for step in steps:
            swap_copy(part, step).wait_send()
        for up, near, gives in ((True, near_above, gives_above), (False, near_below, gives_below)):

            @pl.when(near)
            def _():
                rim_copy(part, up).wait_send()

            @pl.when(gives)
            def _():
                for copy in far_copies(up, part):
                    copy.wait_send()


def hand_over(fine_hbm, coarse_hbm, out_fine_hbm, out_coarse_hbm, fine_ref, coarse_ref, load_sem, store_sem):
    moves = ((fine_hbm, fine_ref, out_fine_hbm), (coarse_hbm, coarse_ref, out_coarse_hbm))
    for i, (source, held, _) in enumerate(moves):
        pltpu.make_async_copy(source, held, load_sem.at[i]).start()
    for i, (source, held, target) in enumerate(moves):
        pltpu.make_async_copy(source, held, load_sem.at[i]).wait()
        pltpu.make_async_copy(held, target, store_sem.at[i]).start()
    for i, (_, held, target) in enumerate(moves):
        pltpu.make_async_copy(held, target, store_sem.at[i]).wait()


def per_device(n_box, n_freq, spectra_fine, spectra_coarse, kernel_table, lists_fine, lists_coarse, live_counts):
    groups, slots = lists_fine.shape
    coarse_groups = lists_coarse.shape[0]
    own = spectra_fine.shape[0]
    rows = groups + 16
    hbm = pl.BlockSpec(memory_space=pltpu.HBM)
    smem = pl.BlockSpec(memory_space=pltpu.SMEM)
    dma = pltpu.SemaphoreType.DMA
    results = (
        jax.ShapeDtypeStruct((groups, 2, 8, LANES), jnp.bfloat16),
        jax.ShapeDtypeStruct((coarse_groups, 2, 8, LANES), jnp.bfloat16),
    )
    result_scratch = [pltpu.VMEM(r.shape, r.dtype) for r in results]
    fine, coarse = pl.pallas_call(
        functools.partial(kernel, n_box, n_freq),
        out_shape=results,
        in_specs=[smem] + [hbm] * 5,
        out_specs=(hbm, hbm),
        scratch_shapes=result_scratch
        + [
            pltpu.VMEM((2 * BANDS, rows, LANES), jnp.float32),
            dma((groups // 16 + 1,)),
            pltpu.VMEM(spectra_fine.shape, jnp.bfloat16),
            pltpu.VMEM(spectra_coarse.shape, jnp.bfloat16),
            pltpu.VMEM(kernel_table.shape, jnp.bfloat16),
            pltpu.VMEM((slots, groups), jnp.int32),
            pltpu.VMEM((coarse_groups, slots), jnp.int32),
            dma((5,)),
            pltpu.VMEM((n_freq, 2 * own, PACK), jnp.bfloat16),
            pltpu.VMEM((16, 16, PACK), jnp.bfloat16),
            pltpu.VMEM((2, slots * rows, WIDE), jnp.bfloat16),
            pltpu.VMEM((2 * BANDS, slots // 2, WIDE, LANES), jnp.bfloat16),
            pltpu.VMEM((slots * rows, WIDE), jnp.bfloat16),
            pltpu.VMEM((slots * rows, WIDE), jnp.bfloat16),
            dma((len(PARTS), n_freq)),
            dma((len(PARTS), n_freq)),
            dma((len(PARTS), 2)),
            dma((len(PARTS), 2)),
            dma((2, len(PARTS), n_freq)),
            dma((2, len(PARTS), 2)),
            pltpu.SemaphoreType.REGULAR((n_freq,)),
            pltpu.SemaphoreType.REGULAR,
        ],
        compiler_params=pltpu.CompilerParams(
            collective_id=0, has_side_effects=True, vmem_limit_bytes=56 * 1024 * 1024
        ),
    )(live_counts, spectra_fine, spectra_coarse, kernel_table, lists_fine.T, lists_coarse)
    return pl.pallas_call(
        hand_over,
        out_shape=results,
        in_specs=[hbm, hbm],
        out_specs=(hbm, hbm),
        scratch_shapes=result_scratch + [dma((2,)), dma((2,))],
        compiler_params=pltpu.CompilerParams(vmem_limit_bytes=60 * 1024 * 1024),
    )(fine, coarse)


def solution(mesh):
    return jax.shard_map(
        functools.partial(per_device, mesh.shape["box"], mesh.shape["freq"]),
        mesh=mesh,
        in_specs=(
            P(("box", "freq"), None, None, None),
            P(("box", "freq"), None, None, None),
            P(None, None, None, None, "freq"),
            P("box", None),
            P("box", None),
            P("box", None),
        ),
        out_specs=(P("box", None, None, "freq"), P("box", None, None, "freq")),
        check_vma=False,
    )
```

```python
import functools

import jax
import jax.numpy as jnp
from jax import lax
from jax.experimental import pallas as pl
from jax.experimental.pallas import tpu as pltpu
from jax.sharding import PartitionSpec as P

RIM_FINE = 16
RIM_COARSE = 2
HALF = 8
LANES = 128
BAND = 16
BANDS = LANES // BAND
PAIRS = BANDS // 2
WIDE = 2 * 8 * BAND
HALF_BAND = BAND // 2
FIRST = LANES
PACK = FIRST + PAIRS * WIDE
PARTS = ((0, FIRST + 2 * WIDE), (FIRST + 2 * WIDE, 2 * WIDE))


def swap_blocks(planes):
    count = len(planes)
    width = LANES // count
    block = lax.broadcasted_iota(jnp.int32, planes[0].shape, 1) // width
    planes = list(planes)
    step = count // 2
    while step:
        upper = (block & step) != 0
        for p in range(count):
            if p & step == 0:
                first, second = planes[p], planes[p + step]
                planes[p] = jnp.where(upper, pltpu.roll(second, width * step, 1), first)
                planes[p + step] = jnp.where(upper, second, pltpu.roll(first, LANES - width * step, 1))
        step //= 2
    return planes


def interleave():
    row = lax.broadcasted_iota(jnp.int32, (WIDE, WIDE), 0)
    lane = lax.broadcasted_iota(jnp.int32, (WIDE, WIDE), 1)
    hit = (row // BAND == lane % BAND) & (row % BAND == lane // BAND)
    return jnp.where(hit, 1.0, 0.0).astype(jnp.bfloat16)


def by_band(parts, permutation):
    planes = []
    for part in parts:
        turned = jnp.swapaxes(part, 0, 1)
        planes.append(swap_blocks([turned[i] for i in range(8)]))
    stacked = jnp.concatenate(
        [jnp.concatenate([planes[0][g], planes[1][g]], axis=1) for g in range(BANDS)], axis=0
    ).astype(jnp.bfloat16)
    return jnp.dot(stacked, permutation, preferred_element_type=jnp.float32).astype(jnp.bfloat16)


def alive(place, count, live):
    lower = live // 2
    return (place < lower) | (place >= count - (live - lower))


def kernel(
    n_box,
    n_freq,
    live_ref,
    fine_hbm,
    coarse_hbm,
    table_hbm,
    lists_fine_hbm,
    lists_coarse_hbm,
    out_fine_hbm,
    out_coarse_hbm,
    out_fine_ref,
    out_coarse_ref,
    sums,
    store_sem,
    fine_ref,
    coarse_ref,
    table_ref,
    lists_fine_ref,
    lists_coarse_ref,
    load_sem,
    outbox,
    held,
    picks,
    weights,
    gathered0,
    gathered1,
    send_sem,
    recv_sem,
    rim_send,
    rim_recv,
    far_send,
    far_recv,
    ready_sem,
    far_ready,
):
    box = lax.axis_index("box")
    col = lax.axis_index("freq")
    above = lax.rem(box + 1, n_box)
    below = lax.rem(box + n_box - 1, n_box)
    slots = table_ref.shape[0]
    groups = lists_fine_ref.shape[1]
    coarse_groups = lists_coarse_ref.shape[0]
    own = fine_ref.shape[0]
    rows = groups + 16
    live_fine = live_ref[0, 0]
    live_coarse = live_ref[0, 1]
    steps = tuple(range(1, n_freq))
    order = (4, 3, 5, 2, 6, 1, 7)

    has_above, has_below = box < n_box - 1, box > 0
    far_above = has_above & (lax.rem(box, HALF) == HALF - 1)
    far_below = has_below & (lax.rem(box, HALF) == 0)
    near_above = has_above & (lax.rem(box, HALF) != HALF - 1)
    near_below = has_below & (lax.rem(box, HALF) != 0)
    gives_above = far_above & (col >= n_freq - 2)
    gives_below = far_below & (col < 2)

    early = lax.rem(box // HALF, 2) == 0
    late = jnp.logical_not(early)
    rank = col

    def signal(semaphore, **device):
        pl.semaphore_signal(semaphore, inc=1, device_id=device)

    loads = [
        pltpu.make_async_copy(source, target, load_sem.at[i])
        for i, (source, target) in enumerate(
            (
                (fine_hbm, fine_ref),
                (coarse_hbm, coarse_ref),
                (lists_fine_hbm, lists_fine_ref),
                (lists_coarse_hbm, lists_coarse_ref),
                (table_hbm, table_ref),
            )
        )
    ]
    for load in loads:
        load.start()

    barrier = pltpu.get_barrier_semaphore()
    for near, other in ((near_above, above), (near_below, below)):

        @pl.when(near)
        def _():
            signal(barrier, box=other)

    for step in steps:

        @pl.when(late | (rank + step < n_freq))
        def _():
            signal(barrier, freq=lax.rem(col + step, n_freq))

    for far, gives, other, giver in (
        (far_above, gives_above, above, 0),
        (far_below, gives_below, below, n_freq - 2),
    ):

        @pl.when(early & far)
        def _():
            for i in range(2):
                signal(barrier, box=other, freq=giver + i)

        @pl.when(early & gives)
        def _():
            for j in range(n_freq):
                signal(barrier, box=other, freq=j)

    late_ready = (
        n_freq
        - 1
        + jnp.where(far_above, 2, 0)
        + jnp.where(far_below, 2, 0)
        + jnp.where(gives_above, n_freq, 0)
        + jnp.where(gives_below, n_freq, 0)
    )
    ready = (
        jnp.where(early, rank, late_ready)
        + near_above.astype(jnp.int32)
        + near_below.astype(jnp.int32)
    )

    permutation = interleave()

    place = col * own + lax.broadcasted_iota(jnp.int32, (own, 8, LANES), 0)
    fine_alive = alive(place, groups, live_fine)
    coarse_alive = alive(jnp.full((16, LANES), col, jnp.int32), coarse_groups, live_coarse)

    def cut(j, carry):
        lanes = pl.ds(pl.multiple_of(j * LANES, LANES), LANES)
        parts = [
            jnp.where(fine_alive, fine_ref[:, c, :, lanes].astype(jnp.float32), 0.0) for c in range(2)
        ]
        bands = by_band(parts, permutation)
        both = jnp.concatenate(
            [coarse_ref[0, c, :, lanes].astype(jnp.float32) for c in range(2)], axis=0
        )
        both = jnp.where(coarse_alive, both, 0.0).astype(jnp.bfloat16)
        rows_of = [bands[16 * pair : 16 * pair + 16] for pair in range(PAIRS)]
        outbox[j] = jnp.concatenate([both, *rows_of], axis=1)
        return carry

    for load in loads[:2]:
        load.wait()
    lax.fori_loop(0, n_freq, cut, 0, unroll=True)

    pl.semaphore_wait(barrier, ready)

    for step in steps:

        @pl.when(early & (rank >= step))
        def _():
            signal(ready_sem.at[step], freq=lax.rem(col + n_freq - step, n_freq))

    for far, other, giver in ((far_above, above, 0), (far_below, below, n_freq - 2)):

        @pl.when(late & far)
        def _():
            for i in range(2):
                signal(far_ready, box=other, freq=giver + i)

    def lanes_of(part):
        return pl.ds(PARTS[part][0], PARTS[part][1])

    def swap_copy(part, step):
        peer = lax.rem(col + step, n_freq)
        return pltpu.make_async_remote_copy(
            src_ref=outbox.at[peer, :, lanes_of(part)],
            dst_ref=held.at[2 + col, :, lanes_of(part)],
            send_sem=send_sem.at[part, step],
            recv_sem=recv_sem.at[part, step],
            device_id={"freq": peer},
        )

    def rim_copy(part, up):
        first, landing = (n_freq, 0) if up else (2, 2 + n_freq)
        return pltpu.make_async_remote_copy(
            src_ref=held.at[pl.ds(first, 2), :, lanes_of(part)],
            dst_ref=held.at[pl.ds(landing, 2), :, lanes_of(part)],
            send_sem=rim_send.at[part, int(up)],
            recv_sem=rim_recv.at[part, int(up)],
            device_id={"box": above if up else below},
        )

    def far_copies(up, part):
        if up:
            other, landing = above, col - (n_freq - 2)
        else:
            other, landing = below, n_freq + 2 + col
        return [
            pltpu.make_async_remote_copy(
                src_ref=outbox.at[j, :, lanes_of(part)],
                dst_ref=held.at[landing, :, lanes_of(part)],
                send_sem=far_send.at[int(up), part, j],
                recv_sem=far_recv.at[int(up), part, lax.rem(col, 2)],
                device_id={"box": other, "freq": j},
            )
            for j in range(n_freq)
        ]

    def far_wait(up, part):
        for i in range(2):
            here = held.at[i if up else n_freq + 2 + i, :, lanes_of(part)]
            pltpu.make_async_copy(here, here, far_recv.at[int(up), part, i]).wait()

    def far_start(when):
        for up, gives in ((True, gives_above), (False, gives_below)):

            @pl.when(when & gives)
            def _():
                for part in range(len(PARTS)):
                    for copy in far_copies(up, part):
                        copy.start()

    far_start(late)
    for part in range(len(PARTS)):
        for first_step, then_step in zip(steps, order):

            @pl.when(early & (rank + first_step >= n_freq))
            def _():
                swap_copy(part, first_step).start()

            @pl.when(late)
            def _():
                swap_copy(part, then_step).start()

    def send_on():
        for step in steps:

            @pl.when(early & (rank + step < n_freq))
            def _():
                pl.semaphore_wait(ready_sem.at[step], 1)
                for part in range(len(PARTS)):
                    swap_copy(part, step).start()

        @pl.when(early & (gives_above | gives_below))
        def _():
            pl.semaphore_wait(far_ready, n_freq)

        far_start(early)

    held[2 + col] = outbox[col]
    blank = jnp.zeros((16, PACK), jnp.bfloat16)
    for i in range(n_freq + 4, 16):
        held[i] = blank

    @pl.when(jnp.logical_not(has_below))
    def _():
        for i in range(2):
            held[i] = blank

    @pl.when(jnp.logical_not(has_above))
    def _():
        for i in range(2):
            held[n_freq + 2 + i] = blank

    def prepare():
        for load in loads[2:]:
            load.wait()
        fine_list = jnp.transpose(lists_fine_ref[...])
        fine_at = fine_list - (box * groups - RIM_FINE)
        fine_row = jnp.where(fine_list >= 0, (fine_at // 8) * 16 + fine_at % 8, -1000)
        coarse_list = lists_coarse_ref[...]
        coarse_at = coarse_list - (box * coarse_groups - RIM_COARSE)
        coarse_row = jnp.where(coarse_list >= 0, 192 + coarse_at, -1000)
        lane_fine = lax.broadcasted_iota(jnp.int32, (groups, WIDE), 1)
        lane_coarse = lax.broadcasted_iota(jnp.int32, (coarse_groups, WIDE), 1)
        no_rows = jnp.zeros((16 - coarse_groups, WIDE), jnp.float32)
        for k in range(slots):
            for odd in range(2):
                picks[odd, pl.ds(k * rows, groups)] = jnp.where(
                    fine_row[:, k : k + 1] + 8 * odd == lane_fine, 1.0, 0.0
                ).astype(jnp.bfloat16)
                coarse_hit = jnp.where(coarse_row[:, k : k + 1] + 16 * odd == lane_coarse, 1.0, 0.0)
                picks[odd, pl.ds(k * rows + groups, 16)] = jnp.concatenate(
                    [coarse_hit, no_rows], axis=0
                ).astype(jnp.bfloat16)

        lane = lax.broadcasted_iota(jnp.int32, (16, LANES), 1) % HALF_BAND
        left = lax.broadcasted_iota(jnp.int32, (8, LANES), 1) < LANES // 2

        def widen(pair, carry):
            for i in range(2):
                planes = [
                    table_ref[2 * pair + i, c, o].astype(jnp.float32)
                    for c in range(2)
                    for o in range(8)
                ]
                for b, real in enumerate(swap_blocks(planes)):
                    turned = pltpu.roll(real, LANES // 2, 1)
                    imag = jnp.where(left, -turned, turned)
                    full = jnp.concatenate([real, imag], axis=0).astype(jnp.bfloat16)
                    for f in range(HALF_BAND):
                        weights[b, pair, pl.ds(i * LANES + f * 16, 16)] = jnp.where(
                            lane == f, full, jnp.zeros_like(full)
                        )
            return carry

        lax.fori_loop(0, slots // 2, widen, 0)

    def middle(turn, carry):
        local = (turn == 0) == (early & (rank < 2))

        @pl.when(local)
        def _():
            prepare()

        @pl.when(jnp.logical_not(local))
        def _():
            send_on()

        return carry

    lax.fori_loop(0, 2, middle, 0)

    def rim_wait(part):
        for up, near, far in ((True, near_below, far_below), (False, near_above, far_above)):

            @pl.when(near)
            def _():
                rim_copy(part, up).wait_recv()

            @pl.when(far)
            def _():
                far_wait(up, part)

    def arrive(part):
        for senders, up, near in (
            ((0, 1), False, near_below),
            ((n_freq - 2, n_freq - 1), True, near_above),
            (range(2, n_freq - 2), None, None),
        ):
            for j in senders:
                step = lax.rem(col + n_freq - j, n_freq)

                @pl.when(step > 0)
                def _():
                    swap_copy(part, step).wait_recv()

            if near is not None:

                @pl.when(near)
                def _():
                    rim_copy(part, up).start()

    arrive(0)
    rim_wait(0)
    raw = held[:, :, pl.ds(0, LANES)].astype(jnp.float32)
    coarse_bands = by_band([raw[:, 0:8], raw[:, 8:16]], permutation)
    for g in range(BANDS):
        held[n_freq + 4 + g % 2, :, pl.ds(FIRST + g // 2 * WIDE, WIDE)] = coarse_bands[16 * g : 16 * g + 16]

    def advance(pair, carry):
        @pl.when(pair == 1)
        def _():
            arrive(1)

        @pl.when(pair == 2)
        def _():
            rim_wait(1)

        lanes = pl.ds(pl.multiple_of(FIRST + pair * WIDE, LANES), WIDE)
        sources = held[:, :, lanes].reshape(16 * 16, WIDE)
        for odd, gathered in enumerate((gathered0, gathered1)):
            for m in range(0, slots * rows, 416):
                gathered[pl.ds(m, 416)] = jnp.dot(
                    picks[odd, pl.ds(m, 416)], sources, preferred_element_type=jnp.float32
                ).astype(jnp.bfloat16)
        for odd, gathered in enumerate((gathered0, gathered1)):
            for half in range(2):
                band = 4 * pair + 2 * odd + half
                side = pl.ds(half * LANES, LANES)
                total = jnp.zeros((rows, LANES), jnp.float32)
                for k in range(0, slots, 2):
                    both = jnp.concatenate(
                        [gathered[pl.ds((k + i) * rows, rows), side] for i in range(2)], axis=1
                    )
                    total = total + jnp.dot(
                        both, weights[band, k // 2], preferred_element_type=jnp.float32
                    )
                sums[band] = total
        return carry

    lax.fori_loop(0, PAIRS, advance, 0)

    def back(first, place, live, count, scale):
        keep = alive(place + lax.broadcasted_iota(jnp.int32, (16, 8, LANES), 0), count, live)
        planes = swap_blocks([sums[b, pl.ds(first, 16)] for b in range(2 * BANDS)])
        result = []
        for c in range(2):
            turned = jnp.swapaxes(jnp.stack(planes[8 * c : 8 * c + 8], axis=0), 0, 1)
            result.append(jnp.where(keep, scale * turned, 0.0).astype(jnp.bfloat16))
        return result

    stores = []
    result = back(groups, 0, live_coarse, coarse_groups, 0.5)
    for c in range(2):
        out_coarse_ref[:, c] = result[c][:coarse_groups]
    stores.append(pltpu.make_async_copy(out_coarse_ref, out_coarse_hbm, store_sem.at[0]))
    stores[-1].start()
    for first in range(0, groups, 16):
        result = back(first, first, live_fine, groups, 1.0)
        part = pl.ds(first, 16)
        for c in range(2):
            out_fine_ref[part, c] = result[c]
        stores.append(
            pltpu.make_async_copy(
                out_fine_ref.at[part], out_fine_hbm.at[part], store_sem.at[first // 16 + 1]
            )
        )
        stores[-1].start()
    for store in stores:
        store.wait()

    for part in range(len(PARTS)):
        for step in steps:
            swap_copy(part, step).wait_send()
        for up, near, gives in ((True, near_above, gives_above), (False, near_below, gives_below)):

            @pl.when(near)
            def _():
                rim_copy(part, up).wait_send()

            @pl.when(gives)
            def _():
                for copy in far_copies(up, part):
                    copy.wait_send()


def hand_over(fine_hbm, coarse_hbm, out_fine_hbm, out_coarse_hbm, fine_ref, coarse_ref, load_sem, store_sem):
    moves = ((fine_hbm, fine_ref, out_fine_hbm), (coarse_hbm, coarse_ref, out_coarse_hbm))
    for i, (source, held, _) in enumerate(moves):
        pltpu.make_async_copy(source, held, load_sem.at[i]).start()
    for i, (source, held, target) in enumerate(moves):
        pltpu.make_async_copy(source, held, load_sem.at[i]).wait()
        pltpu.make_async_copy(held, target, store_sem.at[i]).start()
    for i, (_, held, target) in enumerate(moves):
        pltpu.make_async_copy(held, target, store_sem.at[i]).wait()


def per_device(n_box, n_freq, spectra_fine, spectra_coarse, kernel_table, lists_fine, lists_coarse, live_counts):
    groups, slots = lists_fine.shape
    coarse_groups = lists_coarse.shape[0]
    own = spectra_fine.shape[0]
    rows = groups + 16
    hbm = pl.BlockSpec(memory_space=pltpu.HBM)
    smem = pl.BlockSpec(memory_space=pltpu.SMEM)
    dma = pltpu.SemaphoreType.DMA
    results = (
        jax.ShapeDtypeStruct((groups, 2, 8, LANES), jnp.bfloat16),
        jax.ShapeDtypeStruct((coarse_groups, 2, 8, LANES), jnp.bfloat16),
    )
    result_scratch = [pltpu.VMEM(r.shape, r.dtype) for r in results]
    fine, coarse = pl.pallas_call(
        functools.partial(kernel, n_box, n_freq),
        out_shape=results,
        in_specs=[smem] + [hbm] * 5,
        out_specs=(hbm, hbm),
        scratch_shapes=result_scratch
        + [
            pltpu.VMEM((2 * BANDS, rows, LANES), jnp.float32),
            dma((groups // 16 + 1,)),
            pltpu.VMEM(spectra_fine.shape, jnp.bfloat16),
            pltpu.VMEM(spectra_coarse.shape, jnp.bfloat16),
            pltpu.VMEM(kernel_table.shape, jnp.bfloat16),
            pltpu.VMEM((slots, groups), jnp.int32),
            pltpu.VMEM((coarse_groups, slots), jnp.int32),
            dma((5,)),
            pltpu.VMEM((n_freq, 2 * own, PACK), jnp.bfloat16),
            pltpu.VMEM((16, 16, PACK), jnp.bfloat16),
            pltpu.VMEM((2, slots * rows, WIDE), jnp.bfloat16),
            pltpu.VMEM((2 * BANDS, slots // 2, WIDE, LANES), jnp.bfloat16),
            pltpu.VMEM((slots * rows, WIDE), jnp.bfloat16),
            pltpu.VMEM((slots * rows, WIDE), jnp.bfloat16),
            dma((len(PARTS), n_freq)),
            dma((len(PARTS), n_freq)),
            dma((len(PARTS), 2)),
            dma((len(PARTS), 2)),
            dma((2, len(PARTS), n_freq)),
            dma((2, len(PARTS), 2)),
            pltpu.SemaphoreType.REGULAR((n_freq,)),
            pltpu.SemaphoreType.REGULAR,
        ],
        compiler_params=pltpu.CompilerParams(
            collective_id=0, has_side_effects=True, vmem_limit_bytes=56 * 1024 * 1024
        ),
    )(live_counts, spectra_fine, spectra_coarse, kernel_table, lists_fine.T, lists_coarse)
    return pl.pallas_call(
        hand_over,
        out_shape=results,
        in_specs=[hbm, hbm],
        out_specs=(hbm, hbm),
        scratch_shapes=result_scratch + [dma((2,)), dma((2,))],
        compiler_params=pltpu.CompilerParams(vmem_limit_bytes=60 * 1024 * 1024),
    )(fine, coarse)


def solution(mesh):
    return jax.shard_map(
        functools.partial(per_device, mesh.shape["box"], mesh.shape["freq"]),
        mesh=mesh,
        in_specs=(
            P(("box", "freq"), None, None, None),
            P(("box", "freq"), None, None, None),
            P(None, None, None, None, "freq"),
            P("box", None),
            P("box", None),
            P("box", None),
        ),
        out_specs=(P("box", None, None, "freq"), P("box", None, None, "freq")),
        check_vma=False,
    )
```

```python
import functools

import jax
import jax.numpy as jnp
from jax import lax
from jax.experimental import pallas as pl
from jax.experimental.pallas import tpu as pltpu
from jax.sharding import PartitionSpec as P

RIM_FINE = 16
RIM_COARSE = 2
HALF = 8
LANES = 128
BAND = 16
BANDS = LANES // BAND
PAIRS = BANDS // 2
WIDE = 2 * 8 * BAND
HALF_BAND = BAND // 2
FIRST = LANES
PACK = FIRST + PAIRS * WIDE
PARTS = ((0, FIRST + 2 * WIDE), (FIRST + 2 * WIDE, 2 * WIDE))


def swap_blocks(planes):
    count = len(planes)
    width = LANES // count
    block = lax.broadcasted_iota(jnp.int32, planes[0].shape, 1) // width
    bits = [1 << i for i in range(count.bit_length() - 1)]
    picked = {bit: (block & bit) != 0 for bit in bits}
    planes = list(planes)
    for bit in bits:
        planes = [jnp.where(picked[bit], planes[(p + bit) % count], planes[p]) for p in range(count)]
    planes = [planes[0]] + [pltpu.roll(planes[p], width * p, 1) for p in range(1, count)]
    planes = [planes[-p % count] for p in range(count)]
    for bit in bits:
        planes = [jnp.where(picked[bit], planes[(p - bit) % count], planes[p]) for p in range(count)]
    return planes


def interleave():
    row = lax.broadcasted_iota(jnp.int32, (WIDE, WIDE), 0)
    lane = lax.broadcasted_iota(jnp.int32, (WIDE, WIDE), 1)
    hit = (row // BAND == lane % BAND) & (row % BAND == lane // BAND)
    return jnp.where(hit, 1.0, 0.0).astype(jnp.bfloat16)


def by_band(parts, permutation):
    planes = []
    for part in parts:
        turned = jnp.swapaxes(part, 0, 1)
        planes.append(swap_blocks([turned[i] for i in range(8)]))
    stacked = jnp.concatenate(
        [jnp.concatenate([planes[0][g], planes[1][g]], axis=1) for g in range(BANDS)], axis=0
    ).astype(jnp.bfloat16)
    return jnp.dot(stacked, permutation, preferred_element_type=jnp.float32).astype(jnp.bfloat16)


def alive(place, count, live):
    lower = live // 2
    return (place < lower) | (place >= count - (live - lower))


def kernel(
    n_box,
    n_freq,
    live_ref,
    fine_hbm,
    coarse_hbm,
    table_hbm,
    lists_fine_hbm,
    lists_coarse_hbm,
    out_fine_hbm,
    out_coarse_hbm,
    out_fine_ref,
    out_coarse_ref,
    sums,
    store_sem,
    fine_ref,
    coarse_ref,
    table_ref,
    lists_fine_ref,
    lists_coarse_ref,
    load_sem,
    outbox,
    held,
    picks,
    weights,
    gathered0,
    gathered1,
    send_sem,
    recv_sem,
    rim_send,
    rim_recv,
    far_send,
    far_recv,
    ready_sem,
    far_ready,
):
    box = lax.axis_index("box")
    col = lax.axis_index("freq")
    above = lax.rem(box + 1, n_box)
    below = lax.rem(box + n_box - 1, n_box)
    slots = table_ref.shape[0]
    groups = lists_fine_ref.shape[1]
    coarse_groups = lists_coarse_ref.shape[0]
    own = fine_ref.shape[0]
    rows = groups + 16
    live_fine = live_ref[0, 0]
    live_coarse = live_ref[0, 1]
    steps = tuple(range(1, n_freq))
    order = (4, 3, 5, 2, 6, 1, 7)

    has_above, has_below = box < n_box - 1, box > 0
    far_above = has_above & (lax.rem(box, HALF) == HALF - 1)
    far_below = has_below & (lax.rem(box, HALF) == 0)
    near_above = has_above & (lax.rem(box, HALF) != HALF - 1)
    near_below = has_below & (lax.rem(box, HALF) != 0)
    gives_above = far_above & (col >= n_freq - 2)
    gives_below = far_below & (col < 2)

    early = lax.rem(box // HALF, 2) == 0
    late = jnp.logical_not(early)
    rank = col

    def signal(semaphore, **device):
        pl.semaphore_signal(semaphore, inc=1, device_id=device)

    loads = [
        pltpu.make_async_copy(source, target, load_sem.at[i])
        for i, (source, target) in enumerate(
            (
                (fine_hbm, fine_ref),
                (coarse_hbm, coarse_ref),
                (lists_fine_hbm, lists_fine_ref),
                (lists_coarse_hbm, lists_coarse_ref),
                (table_hbm, table_ref),
            )
        )
    ]
    for load in loads:
        load.start()

    barrier = pltpu.get_barrier_semaphore()
    for near, other in ((near_above, above), (near_below, below)):

        @pl.when(near)
        def _():
            signal(barrier, box=other)

    for step in steps:

        @pl.when(late | (rank + step < n_freq))
        def _():
            signal(barrier, freq=lax.rem(col + step, n_freq))

    for far, gives, other, giver in (
        (far_above, gives_above, above, 0),
        (far_below, gives_below, below, n_freq - 2),
    ):

        @pl.when(early & far)
        def _():
            for i in range(2):
                signal(barrier, box=other, freq=giver + i)

        @pl.when(early & gives)
        def _():
            for j in range(n_freq):
                signal(barrier, box=other, freq=j)

    late_ready = (
        n_freq
        - 1
        + jnp.where(far_above, 2, 0)
        + jnp.where(far_below, 2, 0)
        + jnp.where(gives_above, n_freq, 0)
        + jnp.where(gives_below, n_freq, 0)
    )
    ready = (
        jnp.where(early, rank, late_ready)
        + near_above.astype(jnp.int32)
        + near_below.astype(jnp.int32)
    )

    permutation = interleave()

    place = col * own + lax.broadcasted_iota(jnp.int32, (own, 8, LANES), 0)
    fine_alive = alive(place, groups, live_fine)
    coarse_alive = alive(jnp.full((16, LANES), col, jnp.int32), coarse_groups, live_coarse)

    def cut(j, carry):
        lanes = pl.ds(pl.multiple_of(j * LANES, LANES), LANES)
        parts = [
            jnp.where(fine_alive, fine_ref[:, c, :, lanes].astype(jnp.float32), 0.0) for c in range(2)
        ]
        bands = by_band(parts, permutation)
        both = jnp.concatenate(
            [coarse_ref[0, c, :, lanes].astype(jnp.float32) for c in range(2)], axis=0
        )
        both = jnp.where(coarse_alive, both, 0.0).astype(jnp.bfloat16)
        rows_of = [bands[16 * pair : 16 * pair + 16] for pair in range(PAIRS)]
        outbox[j] = jnp.concatenate([both, *rows_of], axis=1)
        return carry

    for load in loads[:2]:
        load.wait()
    lax.fori_loop(0, n_freq, cut, 0, unroll=True)

    pl.semaphore_wait(barrier, ready)

    for step in steps:

        @pl.when(early & (rank >= step))
        def _():
            signal(ready_sem.at[step], freq=lax.rem(col + n_freq - step, n_freq))

    for far, other, giver in ((far_above, above, 0), (far_below, below, n_freq - 2)):

        @pl.when(late & far)
        def _():
            for i in range(2):
                signal(far_ready, box=other, freq=giver + i)

    def lanes_of(part):
        return pl.ds(PARTS[part][0], PARTS[part][1])

    def swap_copy(part, step):
        peer = lax.rem(col + step, n_freq)
        return pltpu.make_async_remote_copy(
            src_ref=outbox.at[peer, :, lanes_of(part)],
            dst_ref=held.at[2 + col, :, lanes_of(part)],
            send_sem=send_sem.at[part, step],
            recv_sem=recv_sem.at[part, step],
            device_id={"freq": peer},
        )

    def rim_copy(part, up):
        first, landing = (n_freq, 0) if up else (2, 2 + n_freq)
        return pltpu.make_async_remote_copy(
            src_ref=held.at[pl.ds(first, 2), :, lanes_of(part)],
            dst_ref=held.at[pl.ds(landing, 2), :, lanes_of(part)],
            send_sem=rim_send.at[part, int(up)],
            recv_sem=rim_recv.at[part, int(up)],
            device_id={"box": above if up else below},
        )

    def far_copies(up, part):
        if up:
            other, landing = above, col - (n_freq - 2)
        else:
            other, landing = below, n_freq + 2 + col
        return [
            pltpu.make_async_remote_copy(
                src_ref=outbox.at[j, :, lanes_of(part)],
                dst_ref=held.at[landing, :, lanes_of(part)],
                send_sem=far_send.at[int(up), part, j],
                recv_sem=far_recv.at[int(up), part, lax.rem(col, 2)],
                device_id={"box": other, "freq": j},
            )
            for j in range(n_freq)
        ]

    def far_wait(up, part):
        for i in range(2):
            here = held.at[i if up else n_freq + 2 + i, :, lanes_of(part)]
            pltpu.make_async_copy(here, here, far_recv.at[int(up), part, i]).wait()

    def far_start(when):
        for up, gives in ((True, gives_above), (False, gives_below)):

            @pl.when(when & gives)
            def _():
                for part in range(len(PARTS)):
                    for copy in far_copies(up, part):
                        copy.start()

    far_start(late)
    for part in range(len(PARTS)):
        for first_step, then_step in zip(steps, order):

            @pl.when(early & (rank + first_step >= n_freq))
            def _():
                swap_copy(part, first_step).start()

            @pl.when(late)
            def _():
                swap_copy(part, then_step).start()

    def send_on():
        for step in steps:

            @pl.when(early & (rank + step < n_freq))
            def _():
                pl.semaphore_wait(ready_sem.at[step], 1)
                for part in range(len(PARTS)):
                    swap_copy(part, step).start()

        @pl.when(early & (gives_above | gives_below))
        def _():
            pl.semaphore_wait(far_ready, n_freq)

        far_start(early)

    held[2 + col] = outbox[col]
    blank = jnp.zeros((16, PACK), jnp.bfloat16)
    for i in range(n_freq + 4, 16):
        held[i] = blank

    @pl.when(jnp.logical_not(has_below))
    def _():
        for i in range(2):
            held[i] = blank

    @pl.when(jnp.logical_not(has_above))
    def _():
        for i in range(2):
            held[n_freq + 2 + i] = blank

    def prepare():
        for load in loads[2:]:
            load.wait()
        fine_list = jnp.transpose(lists_fine_ref[...])
        fine_at = fine_list - (box * groups - RIM_FINE)
        fine_row = jnp.where(fine_list >= 0, (fine_at // 8) * 16 + fine_at % 8, -1000)
        coarse_list = lists_coarse_ref[...]
        coarse_at = coarse_list - (box * coarse_groups - RIM_COARSE)
        coarse_row = jnp.where(coarse_list >= 0, 192 + coarse_at, -1000)
        lane_fine = lax.broadcasted_iota(jnp.int32, (groups, WIDE), 1)
        lane_coarse = lax.broadcasted_iota(jnp.int32, (coarse_groups, WIDE), 1)
        no_rows = jnp.zeros((16 - coarse_groups, WIDE), jnp.float32)
        for k in range(slots):
            for odd in range(2):
                picks[odd, pl.ds(k * rows, groups)] = jnp.where(
                    fine_row[:, k : k + 1] + 8 * odd == lane_fine, 1.0, 0.0
                ).astype(jnp.bfloat16)
                coarse_hit = jnp.where(coarse_row[:, k : k + 1] + 16 * odd == lane_coarse, 1.0, 0.0)
                picks[odd, pl.ds(k * rows + groups, 16)] = jnp.concatenate(
                    [coarse_hit, no_rows], axis=0
                ).astype(jnp.bfloat16)

        lane = lax.broadcasted_iota(jnp.int32, (16, LANES), 1) % HALF_BAND
        left = lax.broadcasted_iota(jnp.int32, (8, LANES), 1) < LANES // 2

        def widen(pair, carry):
            for i in range(2):
                planes = [
                    table_ref[2 * pair + i, c, o].astype(jnp.float32)
                    for c in range(2)
                    for o in range(8)
                ]
                for b, real in enumerate(swap_blocks(planes)):
                    turned = pltpu.roll(real, LANES // 2, 1)
                    imag = jnp.where(left, -turned, turned)
                    full = jnp.concatenate([real, imag], axis=0).astype(jnp.bfloat16)
                    for f in range(HALF_BAND):
                        weights[b, pair, pl.ds(i * LANES + f * 16, 16)] = jnp.where(
                            lane == f, full, jnp.zeros_like(full)
                        )
            return carry

        lax.fori_loop(0, slots // 2, widen, 0)

    def middle(turn, carry):
        local = (turn == 0) == (early & (rank < 2))

        @pl.when(local)
        def _():
            prepare()

        @pl.when(jnp.logical_not(local))
        def _():
            send_on()

        return carry

    lax.fori_loop(0, 2, middle, 0)

    def rim_wait(part):
        for up, near, far in ((True, near_below, far_below), (False, near_above, far_above)):

            @pl.when(near)
            def _():
                rim_copy(part, up).wait_recv()

            @pl.when(far)
            def _():
                far_wait(up, part)

    def arrive(part):
        for senders, up, near in (
            ((0, 1), False, near_below),
            ((n_freq - 2, n_freq - 1), True, near_above),
            (range(2, n_freq - 2), None, None),
        ):
            for j in senders:
                step = lax.rem(col + n_freq - j, n_freq)

                @pl.when(step > 0)
                def _():
                    swap_copy(part, step).wait_recv()

            if near is not None:

                @pl.when(near)
                def _():
                    rim_copy(part, up).start()

    arrive(0)
    rim_wait(0)
    raw = held[:, :, pl.ds(0, LANES)].astype(jnp.float32)
    coarse_bands = by_band([raw[:, 0:8], raw[:, 8:16]], permutation)
    for g in range(BANDS):
        held[n_freq + 4 + g % 2, :, pl.ds(FIRST + g // 2 * WIDE, WIDE)] = coarse_bands[16 * g : 16 * g + 16]

    def advance(pair, carry):
        @pl.when(pair == 1)
        def _():
            arrive(1)

        @pl.when(pair == 2)
        def _():
            rim_wait(1)

        lanes = pl.ds(pl.multiple_of(FIRST + pair * WIDE, LANES), WIDE)
        sources = held[:, :, lanes].reshape(16 * 16, WIDE)
        for odd, gathered in enumerate((gathered0, gathered1)):
            for m in range(0, slots * rows, 416):
                gathered[pl.ds(m, 416)] = jnp.dot(
                    picks[odd, pl.ds(m, 416)], sources, preferred_element_type=jnp.float32
                ).astype(jnp.bfloat16)
        for odd, gathered in enumerate((gathered0, gathered1)):
            for half in range(2):
                band = 4 * pair + 2 * odd + half
                side = pl.ds(half * LANES, LANES)
                total = jnp.zeros((rows, LANES), jnp.float32)
                for k in range(0, slots, 2):
                    both = jnp.concatenate(
                        [gathered[pl.ds((k + i) * rows, rows), side] for i in range(2)], axis=1
                    )
                    total = total + jnp.dot(
                        both, weights[band, k // 2], preferred_element_type=jnp.float32
                    )
                sums[band] = total
        return carry

    lax.fori_loop(0, PAIRS, advance, 0)

    def back(first, place, live, count, scale):
        keep = alive(place + lax.broadcasted_iota(jnp.int32, (16, 8, LANES), 0), count, live)
        planes = swap_blocks([sums[b, pl.ds(first, 16)] for b in range(2 * BANDS)])
        result = []
        for c in range(2):
            turned = jnp.swapaxes(jnp.stack(planes[8 * c : 8 * c + 8], axis=0), 0, 1)
            result.append(jnp.where(keep, scale * turned, 0.0).astype(jnp.bfloat16))
        return result

    stores = []
    result = back(groups, 0, live_coarse, coarse_groups, 0.5)
    for c in range(2):
        out_coarse_ref[:, c] = result[c][:coarse_groups]
    stores.append(pltpu.make_async_copy(out_coarse_ref, out_coarse_hbm, store_sem.at[0]))
    stores[-1].start()
    for first in range(0, groups, 16):
        result = back(first, first, live_fine, groups, 1.0)
        part = pl.ds(first, 16)
        for c in range(2):
            out_fine_ref[part, c] = result[c]
        stores.append(
            pltpu.make_async_copy(
                out_fine_ref.at[part], out_fine_hbm.at[part], store_sem.at[first // 16 + 1]
            )
        )
        stores[-1].start()
    for store in stores:
        store.wait()

    for part in range(len(PARTS)):
        for step in steps:
            swap_copy(part, step).wait_send()
        for up, near, gives in ((True, near_above, gives_above), (False, near_below, gives_below)):

            @pl.when(near)
            def _():
                rim_copy(part, up).wait_send()

            @pl.when(gives)
            def _():
                for copy in far_copies(up, part):
                    copy.wait_send()


def hand_over(fine_hbm, coarse_hbm, out_fine_hbm, out_coarse_hbm, fine_ref, coarse_ref, load_sem, store_sem):
    moves = ((fine_hbm, fine_ref, out_fine_hbm), (coarse_hbm, coarse_ref, out_coarse_hbm))
    for i, (source, held, _) in enumerate(moves):
        pltpu.make_async_copy(source, held, load_sem.at[i]).start()
    for i, (source, held, target) in enumerate(moves):
        pltpu.make_async_copy(source, held, load_sem.at[i]).wait()
        pltpu.make_async_copy(held, target, store_sem.at[i]).start()
    for i, (_, held, target) in enumerate(moves):
        pltpu.make_async_copy(held, target, store_sem.at[i]).wait()


def per_device(n_box, n_freq, spectra_fine, spectra_coarse, kernel_table, lists_fine, lists_coarse, live_counts):
    groups, slots = lists_fine.shape
    coarse_groups = lists_coarse.shape[0]
    own = spectra_fine.shape[0]
    rows = groups + 16
    hbm = pl.BlockSpec(memory_space=pltpu.HBM)
    smem = pl.BlockSpec(memory_space=pltpu.SMEM)
    dma = pltpu.SemaphoreType.DMA
    results = (
        jax.ShapeDtypeStruct((groups, 2, 8, LANES), jnp.bfloat16),
        jax.ShapeDtypeStruct((coarse_groups, 2, 8, LANES), jnp.bfloat16),
    )
    result_scratch = [pltpu.VMEM(r.shape, r.dtype) for r in results]
    fine, coarse = pl.pallas_call(
        functools.partial(kernel, n_box, n_freq),
        out_shape=results,
        in_specs=[smem] + [hbm] * 5,
        out_specs=(hbm, hbm),
        scratch_shapes=result_scratch
        + [
            pltpu.VMEM((2 * BANDS, rows, LANES), jnp.float32),
            dma((groups // 16 + 1,)),
            pltpu.VMEM(spectra_fine.shape, jnp.bfloat16),
            pltpu.VMEM(spectra_coarse.shape, jnp.bfloat16),
            pltpu.VMEM(kernel_table.shape, jnp.bfloat16),
            pltpu.VMEM((slots, groups), jnp.int32),
            pltpu.VMEM((coarse_groups, slots), jnp.int32),
            dma((5,)),
            pltpu.VMEM((n_freq, 2 * own, PACK), jnp.bfloat16),
            pltpu.VMEM((16, 16, PACK), jnp.bfloat16),
            pltpu.VMEM((2, slots * rows, WIDE), jnp.bfloat16),
            pltpu.VMEM((2 * BANDS, slots // 2, WIDE, LANES), jnp.bfloat16),
            pltpu.VMEM((slots * rows, WIDE), jnp.bfloat16),
            pltpu.VMEM((slots * rows, WIDE), jnp.bfloat16),
            dma((len(PARTS), n_freq)),
            dma((len(PARTS), n_freq)),
            dma((len(PARTS), 2)),
            dma((len(PARTS), 2)),
            dma((2, len(PARTS), n_freq)),
            dma((2, len(PARTS), 2)),
            pltpu.SemaphoreType.REGULAR((n_freq,)),
            pltpu.SemaphoreType.REGULAR,
        ],
        compiler_params=pltpu.CompilerParams(
            collective_id=0, has_side_effects=True, vmem_limit_bytes=56 * 1024 * 1024
        ),
    )(live_counts, spectra_fine, spectra_coarse, kernel_table, lists_fine.T, lists_coarse)
    return pl.pallas_call(
        hand_over,
        out_shape=results,
        in_specs=[hbm, hbm],
        out_specs=(hbm, hbm),
        scratch_shapes=result_scratch + [dma((2,)), dma((2,))],
        compiler_params=pltpu.CompilerParams(vmem_limit_bytes=60 * 1024 * 1024),
    )(fine, coarse)


def solution(mesh):
    return jax.shard_map(
        functools.partial(per_device, mesh.shape["box"], mesh.shape["freq"]),
        mesh=mesh,
        in_specs=(
            P(("box", "freq"), None, None, None),
            P(("box", "freq"), None, None, None),
            P(None, None, None, None, "freq"),
            P("box", None),
            P("box", None),
            P("box", None),
        ),
        out_specs=(P("box", None, None, "freq"), P("box", None, None, "freq")),
        check_vma=False,
    )
```

```python
import functools

import jax
import jax.numpy as jnp
from jax import lax
from jax.experimental import pallas as pl
from jax.experimental.pallas import tpu as pltpu
from jax.sharding import PartitionSpec as P

RIM_FINE = 16
RIM_COARSE = 2
HALF = 8
LANES = 128
BAND = 16
BANDS = LANES // BAND
PAIRS = BANDS // 2
WIDE = 2 * 8 * BAND
HALF_BAND = BAND // 2
FIRST = LANES
PACK = FIRST + PAIRS * WIDE
PARTS = ((0, FIRST + 2 * WIDE), (FIRST + 2 * WIDE, 2 * WIDE))


def swap_blocks(planes):
    count = len(planes)
    width = LANES // count
    block = lax.broadcasted_iota(jnp.int32, planes[0].shape, 1) // width
    bits = [1 << i for i in range(count.bit_length() - 1)]
    picked = {bit: (block & bit) != 0 for bit in bits}
    planes = list(planes)
    for bit in bits:
        planes = [jnp.where(picked[bit], planes[(p + bit) % count], planes[p]) for p in range(count)]
    planes = [planes[0]] + [pltpu.roll(planes[p], width * p, 1) for p in range(1, count)]
    planes = [planes[-p % count] for p in range(count)]
    for bit in bits:
        planes = [jnp.where(picked[bit], planes[(p - bit) % count], planes[p]) for p in range(count)]
    return planes


def interleave():
    row = lax.broadcasted_iota(jnp.int32, (WIDE, WIDE), 0)
    lane = lax.broadcasted_iota(jnp.int32, (WIDE, WIDE), 1)
    hit = (row // BAND == lane % BAND) & (row % BAND == lane // BAND)
    return jnp.where(hit, 1.0, 0.0).astype(jnp.bfloat16)


def by_band(parts, permutation):
    planes = []
    for part in parts:
        turned = jnp.swapaxes(part, 0, 1)
        planes.append(swap_blocks([turned[i] for i in range(8)]))
    stacked = jnp.concatenate(
        [jnp.concatenate([planes[0][g], planes[1][g]], axis=1) for g in range(BANDS)], axis=0
    ).astype(jnp.bfloat16)
    return jnp.dot(stacked, permutation, preferred_element_type=jnp.float32).astype(jnp.bfloat16)


def alive(place, count, live):
    lower = live // 2
    return (place < lower) | (place >= count - (live - lower))


def kernel(
    n_box,
    n_freq,
    live_ref,
    fine_hbm,
    coarse_hbm,
    table_hbm,
    lists_fine_hbm,
    lists_coarse_hbm,
    out_fine_hbm,
    out_coarse_hbm,
    out_fine_ref,
    out_coarse_ref,
    sums,
    store_sem,
    fine_ref,
    coarse_ref,
    table_ref,
    lists_fine_ref,
    lists_coarse_ref,
    load_sem,
    outbox,
    held,
    picks,
    weights,
    gathered0,
    gathered1,
    send_sem,
    recv_sem,
    rim_send,
    rim_recv,
    far_send,
    far_recv,
    ready_sem,
    far_ready,
):
    box = lax.axis_index("box")
    col = lax.axis_index("freq")
    above = lax.rem(box + 1, n_box)
    below = lax.rem(box + n_box - 1, n_box)
    slots = table_ref.shape[0]
    groups = lists_fine_ref.shape[1]
    coarse_groups = lists_coarse_ref.shape[0]
    own = fine_ref.shape[0]
    rows = groups + 16
    live_fine = live_ref[0, 0]
    live_coarse = live_ref[0, 1]
    steps = tuple(range(1, n_freq))

    has_above, has_below = box < n_box - 1, box > 0
    far_above = has_above & (lax.rem(box, HALF) == HALF - 1)
    far_below = has_below & (lax.rem(box, HALF) == 0)
    near_above = has_above & (lax.rem(box, HALF) != HALF - 1)
    near_below = has_below & (lax.rem(box, HALF) != 0)
    gives_above = far_above & (col >= n_freq - 2)
    gives_below = far_below & (col < 2)

    early = lax.rem(box // HALF, 2) == 0
    late = jnp.logical_not(early)
    rank = col

    def signal(semaphore, **device):
        pl.semaphore_signal(semaphore, inc=1, device_id=device)

    loads = [
        pltpu.make_async_copy(source, target, load_sem.at[i])
        for i, (source, target) in enumerate(
            (
                (fine_hbm, fine_ref),
                (coarse_hbm, coarse_ref),
                (lists_fine_hbm, lists_fine_ref),
                (lists_coarse_hbm, lists_coarse_ref),
                (table_hbm, table_ref),
            )
        )
    ]
    for load in loads:
        load.start()

    barrier = pltpu.get_barrier_semaphore()
    for near, other in ((near_above, above), (near_below, below)):

        @pl.when(near)
        def _():
            signal(barrier, box=other)

    for step in steps:

        @pl.when(late | (rank + step < n_freq))
        def _():
            signal(barrier, freq=lax.rem(col + step, n_freq))

    for far, gives, other, giver in (
        (far_above, gives_above, above, 0),
        (far_below, gives_below, below, n_freq - 2),
    ):

        @pl.when(early & far)
        def _():
            for i in range(2):
                signal(barrier, box=other, freq=giver + i)

        @pl.when(early & gives)
        def _():
            for j in range(n_freq):
                signal(barrier, box=other, freq=j)

    late_ready = (
        n_freq
        - 1
        + jnp.where(far_above, 2, 0)
        + jnp.where(far_below, 2, 0)
        + jnp.where(gives_above, n_freq, 0)
        + jnp.where(gives_below, n_freq, 0)
    )
    ready = (
        jnp.where(early, rank, late_ready)
        + near_above.astype(jnp.int32)
        + near_below.astype(jnp.int32)
    )

    permutation = interleave()

    place = col * own + lax.broadcasted_iota(jnp.int32, (own, 8, LANES), 0)
    fine_alive = alive(place, groups, live_fine)
    coarse_alive = alive(jnp.full((16, LANES), col, jnp.int32), coarse_groups, live_coarse)

    def cut(j, carry):
        lanes = pl.ds(pl.multiple_of(j * LANES, LANES), LANES)
        parts = [
            jnp.where(fine_alive, fine_ref[:, c, :, lanes].astype(jnp.float32), 0.0) for c in range(2)
        ]
        bands = by_band(parts, permutation)
        both = jnp.concatenate(
            [coarse_ref[0, c, :, lanes].astype(jnp.float32) for c in range(2)], axis=0
        )
        both = jnp.where(coarse_alive, both, 0.0).astype(jnp.bfloat16)
        rows_of = [bands[16 * pair : 16 * pair + 16] for pair in range(PAIRS)]
        outbox[j] = jnp.concatenate([both, *rows_of], axis=1)
        return carry

    for load in loads[:2]:
        load.wait()
    lax.fori_loop(0, n_freq, cut, 0, unroll=True)

    pl.semaphore_wait(barrier, ready)

    for step in steps:

        @pl.when(early & (rank >= step))
        def _():
            signal(ready_sem.at[step], freq=lax.rem(col + n_freq - step, n_freq))

    for far, other, giver in ((far_above, above, 0), (far_below, below, n_freq - 2)):

        @pl.when(late & far)
        def _():
            for i in range(2):
                signal(far_ready, box=other, freq=giver + i)

    def lanes_of(part):
        return pl.ds(PARTS[part][0], PARTS[part][1])

    def swap_copy(part, step):
        peer = lax.rem(col + step, n_freq)
        return pltpu.make_async_remote_copy(
            src_ref=outbox.at[peer, :, lanes_of(part)],
            dst_ref=held.at[2 + col, :, lanes_of(part)],
            send_sem=send_sem.at[part, step],
            recv_sem=recv_sem.at[part, step],
            device_id={"freq": peer},
        )

    def rim_copy(part, up):
        first, landing = (n_freq, 0) if up else (2, 2 + n_freq)
        return pltpu.make_async_remote_copy(
            src_ref=held.at[pl.ds(first, 2), :, lanes_of(part)],
            dst_ref=held.at[pl.ds(landing, 2), :, lanes_of(part)],
            send_sem=rim_send.at[part, int(up)],
            recv_sem=rim_recv.at[part, int(up)],
            device_id={"box": above if up else below},
        )

    def far_copies(up, part):
        if up:
            other, landing = above, col - (n_freq - 2)
        else:
            other, landing = below, n_freq + 2 + col
        return [
            pltpu.make_async_remote_copy(
                src_ref=outbox.at[j, :, lanes_of(part)],
                dst_ref=held.at[landing, :, lanes_of(part)],
                send_sem=far_send.at[int(up), part, j],
                recv_sem=far_recv.at[int(up), part, lax.rem(col, 2)],
                device_id={"box": other, "freq": j},
            )
            for j in range(n_freq)
        ]

    def far_wait(up, part):
        for i in range(2):
            here = held.at[i if up else n_freq + 2 + i, :, lanes_of(part)]
            pltpu.make_async_copy(here, here, far_recv.at[int(up), part, i]).wait()

    def far_start(when):
        for up, gives in ((True, gives_above), (False, gives_below)):

            @pl.when(when & gives)
            def _():
                for part in range(len(PARTS)):
                    for copy in far_copies(up, part):
                        copy.start()

    far_start(late)
    for part in range(len(PARTS)):
        for step in steps:

            @pl.when(early & (rank + step >= n_freq))
            def _():
                swap_copy(part, step).start()

        for peer in (4, 5, 6, 7, 3, 2, 1, 0):
            step = lax.rem(peer + jnp.where(col < 4, 0, 4) + n_freq - col, n_freq)

            @pl.when(late & (step > 0))
            def _():
                swap_copy(part, step).start()

    def send_on():
        for step in steps:

            @pl.when(early & (rank + step < n_freq))
            def _():
                pl.semaphore_wait(ready_sem.at[step], 1)
                for part in range(len(PARTS)):
                    swap_copy(part, step).start()

        @pl.when(early & (gives_above | gives_below))
        def _():
            pl.semaphore_wait(far_ready, n_freq)

        far_start(early)

    held[2 + col] = outbox[col]
    blank = jnp.zeros((16, PACK), jnp.bfloat16)
    for i in range(n_freq + 4, 16):
        held[i] = blank

    @pl.when(jnp.logical_not(has_below))
    def _():
        for i in range(2):
            held[i] = blank

    @pl.when(jnp.logical_not(has_above))
    def _():
        for i in range(2):
            held[n_freq + 2 + i] = blank

    def prepare():
        for load in loads[2:]:
            load.wait()
        fine_list = jnp.transpose(lists_fine_ref[...])
        fine_at = fine_list - (box * groups - RIM_FINE)
        fine_row = jnp.where(fine_list >= 0, (fine_at // 8) * 16 + fine_at % 8, -1000)
        coarse_list = lists_coarse_ref[...]
        coarse_at = coarse_list - (box * coarse_groups - RIM_COARSE)
        coarse_row = jnp.where(coarse_list >= 0, 192 + coarse_at, -1000)
        lane_fine = lax.broadcasted_iota(jnp.int32, (groups, WIDE), 1)
        lane_coarse = lax.broadcasted_iota(jnp.int32, (coarse_groups, WIDE), 1)
        no_rows = jnp.zeros((16 - coarse_groups, WIDE), jnp.float32)
        for k in range(slots):
            for odd in range(2):
                picks[odd, pl.ds(k * rows, groups)] = jnp.where(
                    fine_row[:, k : k + 1] + 8 * odd == lane_fine, 1.0, 0.0
                ).astype(jnp.bfloat16)
                coarse_hit = jnp.where(coarse_row[:, k : k + 1] + 16 * odd == lane_coarse, 1.0, 0.0)
                picks[odd, pl.ds(k * rows + groups, 16)] = jnp.concatenate(
                    [coarse_hit, no_rows], axis=0
                ).astype(jnp.bfloat16)

        lane = lax.broadcasted_iota(jnp.int32, (16, LANES), 1) % HALF_BAND
        left = lax.broadcasted_iota(jnp.int32, (8, LANES), 1) < LANES // 2

        def widen(pair, carry):
            for i in range(2):
                planes = [
                    table_ref[2 * pair + i, c, o].astype(jnp.float32)
                    for c in range(2)
                    for o in range(8)
                ]
                for b, real in enumerate(swap_blocks(planes)):
                    turned = pltpu.roll(real, LANES // 2, 1)
                    imag = jnp.where(left, -turned, turned)
                    full = jnp.concatenate([real, imag], axis=0).astype(jnp.bfloat16)
                    for f in range(HALF_BAND):
                        weights[b, pair, pl.ds(i * LANES + f * 16, 16)] = jnp.where(
                            lane == f, full, jnp.zeros_like(full)
                        )
            return carry

        lax.fori_loop(0, slots // 2, widen, 0)

    def middle(turn, carry):
        local = (turn == 0) == (early & (rank < 2))

        @pl.when(local)
        def _():
            prepare()

        @pl.when(jnp.logical_not(local))
        def _():
            send_on()

        return carry

    lax.fori_loop(0, 2, middle, 0)

    def rim_wait(part):
        for up, near, far in ((True, near_below, far_below), (False, near_above, far_above)):

            @pl.when(near)
            def _():
                rim_copy(part, up).wait_recv()

            @pl.when(far)
            def _():
                far_wait(up, part)

    def arrive(part):
        for senders, up, near in (
            ((0, 1), False, near_below),
            ((n_freq - 2, n_freq - 1), True, near_above),
            (range(2, n_freq - 2), None, None),
        ):
            for j in senders:
                step = lax.rem(col + n_freq - j, n_freq)

                @pl.when(step > 0)
                def _():
                    swap_copy(part, step).wait_recv()

            if near is not None:

                @pl.when(near)
                def _():
                    rim_copy(part, up).start()

    arrive(0)
    rim_wait(0)
    raw = held[:, :, pl.ds(0, LANES)].astype(jnp.float32)
    coarse_bands = by_band([raw[:, 0:8], raw[:, 8:16]], permutation)
    for g in range(BANDS):
        held[n_freq + 4 + g % 2, :, pl.ds(FIRST + g // 2 * WIDE, WIDE)] = coarse_bands[16 * g : 16 * g + 16]

    def advance(pair, carry):
        @pl.when(pair == 1)
        def _():
            arrive(1)

        @pl.when(pair == 2)
        def _():
            rim_wait(1)

        lanes = pl.ds(pl.multiple_of(FIRST + pair * WIDE, LANES), WIDE)
        sources = held[:, :, lanes].reshape(16 * 16, WIDE)
        for odd, gathered in enumerate((gathered0, gathered1)):
            for m in range(0, slots * rows, 416):
                gathered[pl.ds(m, 416)] = jnp.dot(
                    picks[odd, pl.ds(m, 416)], sources, preferred_element_type=jnp.float32
                ).astype(jnp.bfloat16)
        for odd, gathered in enumerate((gathered0, gathered1)):
            for half in range(2):
                band = 4 * pair + 2 * odd + half
                side = pl.ds(half * LANES, LANES)
                total = jnp.zeros((rows, LANES), jnp.float32)
                for k in range(0, slots, 2):
                    both = jnp.concatenate(
                        [gathered[pl.ds((k + i) * rows, rows), side] for i in range(2)], axis=1
                    )
                    total = total + jnp.dot(
                        both, weights[band, k // 2], preferred_element_type=jnp.float32
                    )
                sums[band] = total
        return carry

    lax.fori_loop(0, PAIRS, advance, 0)

    def back(first, place, live, count, scale):
        keep = alive(place + lax.broadcasted_iota(jnp.int32, (16, 8, LANES), 0), count, live)
        planes = swap_blocks([sums[b, pl.ds(first, 16)] for b in range(2 * BANDS)])
        result = []
        for c in range(2):
            turned = jnp.swapaxes(jnp.stack(planes[8 * c : 8 * c + 8], axis=0), 0, 1)
            result.append(jnp.where(keep, scale * turned, 0.0).astype(jnp.bfloat16))
        return result

    stores = []
    result = back(groups, 0, live_coarse, coarse_groups, 0.5)
    for c in range(2):
        out_coarse_ref[:, c] = result[c][:coarse_groups]
    stores.append(pltpu.make_async_copy(out_coarse_ref, out_coarse_hbm, store_sem.at[0]))
    stores[-1].start()
    for first in range(0, groups, 16):
        result = back(first, first, live_fine, groups, 1.0)
        part = pl.ds(first, 16)
        for c in range(2):
            out_fine_ref[part, c] = result[c]
        stores.append(
            pltpu.make_async_copy(
                out_fine_ref.at[part], out_fine_hbm.at[part], store_sem.at[first // 16 + 1]
            )
        )
        stores[-1].start()
    for store in stores:
        store.wait()

    for part in range(len(PARTS)):
        for step in steps:
            swap_copy(part, step).wait_send()
        for up, near, gives in ((True, near_above, gives_above), (False, near_below, gives_below)):

            @pl.when(near)
            def _():
                rim_copy(part, up).wait_send()

            @pl.when(gives)
            def _():
                for copy in far_copies(up, part):
                    copy.wait_send()


def hand_over(fine_hbm, coarse_hbm, out_fine_hbm, out_coarse_hbm, fine_ref, coarse_ref, load_sem, store_sem):
    moves = ((fine_hbm, fine_ref, out_fine_hbm), (coarse_hbm, coarse_ref, out_coarse_hbm))
    for i, (source, held, _) in enumerate(moves):
        pltpu.make_async_copy(source, held, load_sem.at[i]).start()
    for i, (source, held, target) in enumerate(moves):
        pltpu.make_async_copy(source, held, load_sem.at[i]).wait()
        pltpu.make_async_copy(held, target, store_sem.at[i]).start()
    for i, (_, held, target) in enumerate(moves):
        pltpu.make_async_copy(held, target, store_sem.at[i]).wait()


def per_device(n_box, n_freq, spectra_fine, spectra_coarse, kernel_table, lists_fine, lists_coarse, live_counts):
    groups, slots = lists_fine.shape
    coarse_groups = lists_coarse.shape[0]
    own = spectra_fine.shape[0]
    rows = groups + 16
    hbm = pl.BlockSpec(memory_space=pltpu.HBM)
    smem = pl.BlockSpec(memory_space=pltpu.SMEM)
    dma = pltpu.SemaphoreType.DMA
    results = (
        jax.ShapeDtypeStruct((groups, 2, 8, LANES), jnp.bfloat16),
        jax.ShapeDtypeStruct((coarse_groups, 2, 8, LANES), jnp.bfloat16),
    )
    result_scratch = [pltpu.VMEM(r.shape, r.dtype) for r in results]
    fine, coarse = pl.pallas_call(
        functools.partial(kernel, n_box, n_freq),
        out_shape=results,
        in_specs=[smem] + [hbm] * 5,
        out_specs=(hbm, hbm),
        scratch_shapes=result_scratch
        + [
            pltpu.VMEM((2 * BANDS, rows, LANES), jnp.float32),
            dma((groups // 16 + 1,)),
            pltpu.VMEM(spectra_fine.shape, jnp.bfloat16),
            pltpu.VMEM(spectra_coarse.shape, jnp.bfloat16),
            pltpu.VMEM(kernel_table.shape, jnp.bfloat16),
            pltpu.VMEM((slots, groups), jnp.int32),
            pltpu.VMEM((coarse_groups, slots), jnp.int32),
            dma((5,)),
            pltpu.VMEM((n_freq, 2 * own, PACK), jnp.bfloat16),
            pltpu.VMEM((16, 16, PACK), jnp.bfloat16),
            pltpu.VMEM((2, slots * rows, WIDE), jnp.bfloat16),
            pltpu.VMEM((2 * BANDS, slots // 2, WIDE, LANES), jnp.bfloat16),
            pltpu.VMEM((slots * rows, WIDE), jnp.bfloat16),
            pltpu.VMEM((slots * rows, WIDE), jnp.bfloat16),
            dma((len(PARTS), n_freq)),
            dma((len(PARTS), n_freq)),
            dma((len(PARTS), 2)),
            dma((len(PARTS), 2)),
            dma((2, len(PARTS), n_freq)),
            dma((2, len(PARTS), 2)),
            pltpu.SemaphoreType.REGULAR((n_freq,)),
            pltpu.SemaphoreType.REGULAR,
        ],
        compiler_params=pltpu.CompilerParams(
            collective_id=0, has_side_effects=True, vmem_limit_bytes=56 * 1024 * 1024
        ),
    )(live_counts, spectra_fine, spectra_coarse, kernel_table, lists_fine.T, lists_coarse)
    return pl.pallas_call(
        hand_over,
        out_shape=results,
        in_specs=[hbm, hbm],
        out_specs=(hbm, hbm),
        scratch_shapes=result_scratch + [dma((2,)), dma((2,))],
        compiler_params=pltpu.CompilerParams(vmem_limit_bytes=60 * 1024 * 1024),
    )(fine, coarse)


def solution(mesh):
    return jax.shard_map(
        functools.partial(per_device, mesh.shape["box"], mesh.shape["freq"]),
        mesh=mesh,
        in_specs=(
            P(("box", "freq"), None, None, None),
            P(("box", "freq"), None, None, None),
            P(None, None, None, None, "freq"),
            P("box", None),
            P("box", None),
            P("box", None),
        ),
        out_specs=(P("box", None, None, "freq"), P("box", None, None, "freq")),
        check_vma=False,
    )
```
